512 devices in a mesh: dp: 32 (over x, z), ctx: 16 (over y, core).
Axes of the slice: x: 4, y: 8, z: 8, core: 2. Of those that a mesh axis runs over, the one named last changes fastest.
Arguments:
- ssm_input: bfloat16 [65536, 4096], P(('dp', 'ctx')), parts along dimension 0, may hold values from -6 to 6
- gate_input: bfloat16 [65536, 4096], P(('dp', 'ctx')), parts along dimension 0, may hold values from -6 to 6
- b_proj: bfloat16 [65536, 512], P(('dp', 'ctx')), parts along dimension 0, may hold values from -0.1796875 to 0.1796875
- c_proj: bfloat16 [65536, 512], P(('dp', 'ctx')), parts along dimension 0, may hold values from -6 to 6
- dt_raw: float32 [65536, 64], P(('dp', 'ctx')), parts along dimension 0, may hold values from -3 to 3
- a_log: float32 [64], replicated, may hold values from -12 to -3
- skip: float32 [64], replicated, may hold values from 1 to 3
- norm_gain: float32 [4096], replicated, may hold values from 0.5 to 1.5
- queries: bfloat16 [65536, 2048], P(('dp', 'ctx')), parts along dimension 0, may hold values from -110 to 110
- keys: bfloat16 [65536, 512], P(('dp', 'ctx')), parts along dimension 0, may hold values from -5 to 5
- values: bfloat16 [65536, 512], P(('dp', 'ctx')), parts along dimension 0, may hold values from -6 to 6
- block_lists: int32 [512, 3], P(('dp', 'ctx')), parts along dimension 0, may hold values from -1 to 14, as said below
Outputs:
- ssm_out: bfloat16 [65536, 4096], P(('dp', 'ctx')), parts along dimension 0
- attn_out: bfloat16 [65536, 2048], P(('dp', 'ctx')), parts along dimension 0
The draws below stay inside these ranges and needn't reach their ends.
There are 32 independent parts, one for each index of `dp`. The reference program is written for one: setup_inputs(seed, part) draws one part's arguments, and reference() takes and returns one part's arrays. A program takes and returns all parts, laid end to end along the dimension named above; an argument that names none is the same for every part. Nothing has to cross between parts.
Inputs may be any that keep to these rules, and one draw needn't show every extreme that they name: `block_lists`: row b lists distinct key blocks below b in its first slots and -1 in the others; every row b >= 1 lists at least one; the last row fills all 3 slots and lists 16 - 2; row 0 lists none.
All inputs are finite; a program needn't handle non-finite values.
Results may differ from the reference program's by a relative error of at most 0.015.
Values may be sent and summed in bfloat16 or wider, within the bound.
A program may use at most 192 MiB of HBM per device.

```python
import jax
import jax.numpy as jnp
from jax import lax

SSM_HEADS = 64
HEAD_P = 64
STATE = 128
GROUPS = 4
QHEADS = 16
KVHEADS = 4
HEAD_D = 128
BLK = 128
KSEL = 3
TOK_DEV = 128
SEQ = 2048
NB = 16


def draw_a_log(key, part):
    key = jax.random.fold_in(key, 1)
    first_key, second_key = jax.random.split(key)
    quick_share = 0.5
    quick = jax.random.uniform(first_key, (SSM_HEADS,), jnp.float32) < quick_share
    spread = jax.random.uniform(second_key, (SSM_HEADS,), jnp.float32)
    fast_log = jnp.log(1.0 / 50.0) + spread * jnp.log(2.0)
    slow_log = jnp.log(0.2 / SEQ) + spread * jnp.log(5.0)
    return jnp.where(quick, fast_log, slow_log).astype(jnp.float32)


def draw_dt_raw(key, part):
    key = jax.random.fold_in(key, 2)
    first_key, second_key = jax.random.split(key)
    base = jax.random.uniform(first_key, (SEQ // TOK_DEV, TOK_DEV, SSM_HEADS), jnp.float32, -1.5, 1.5)
    offset = jax.random.uniform(second_key, (SEQ // TOK_DEV, 1, SSM_HEADS), jnp.float32, -0.7, 0.7)
    return (base + offset).reshape(SEQ, SSM_HEADS).astype(jnp.float32)


def key_base(key):
    return jnp.clip(jax.random.normal(key, (SEQ, KVHEADS * HEAD_D), jnp.float32), -4.5, 4.5)


def listed_blocks(key):
    key = jax.random.fold_in(key, 3)
    first_key, second_key = jax.random.split(key)
    row_ids = jnp.arange(NB, dtype=jnp.int32)[:, None]
    col_ids = jnp.arange(NB, dtype=jnp.int32)[None, :]
    ranking = jax.random.randint(first_key, (NB, NB), 0, 1 << 16, jnp.int32) * NB + col_ids
    ranking = jnp.where(col_ids < row_ids, ranking, -1)
    ranking = jnp.where((row_ids == NB - 1) & (col_ids == NB - 2), (1 << 16) * NB + NB, ranking)
    _, picked = lax.top_k(ranking, KSEL)
    limit = jnp.minimum(row_ids[:, 0], KSEL)
    count_used = 1 + jax.random.randint(second_key, (NB,), 0, 1 << 16, jnp.int32) % jnp.maximum(limit, 1)
    count_used = jnp.minimum(count_used, limit)
    count_used = jnp.where(row_ids[:, 0] == NB - 1, KSEL, count_used)
    slot_ids = jnp.arange(KSEL, dtype=jnp.int32)[None, :]
    return jnp.where(slot_ids < count_used[:, None], picked.astype(jnp.int32), -1).astype(jnp.int32)


def draw_keys(key, part):
    base = key_base(key)
    return base.astype(jnp.bfloat16)


def draw_queries(key, part):
    key = jax.random.fold_in(key, 5)
    fresh = jnp.clip(jax.random.normal(key, (SEQ, QHEADS * HEAD_D), jnp.float32), -4.5, 4.5)
    return fresh.astype(jnp.bfloat16)


def draw_block_lists(key, part):
    return listed_blocks(key)


def block_levels(rng, dims, cuts, low, largest):
    factor_of, own = 1.0, jax.random.fold_in(rng, 6)
    for dim, blocks in cuts:
        draws = jnp.exp(jax.random.uniform(jax.random.fold_in(own, dim), (blocks,), jnp.float32, low / len(cuts), largest / len(cuts)))
        factor_of = factor_of * jnp.repeat(draws, dims[dim] // blocks).reshape([-1 if axis == dim else 1 for axis in range(len(dims))])
    return factor_of


def centred(stream_key, dims, scale, reach, cuts=(), kind=jnp.bfloat16):
    drawn = jax.random.normal(stream_key, dims, jnp.float32) * scale
    if len(cuts) > 0:
        drawn = block_levels(stream_key, dims, cuts, -0.22, 0.18) * drawn
    return jnp.clip(drawn, min=-reach, max=reach).astype(kind)


def setup_inputs(seed: int = 0, part: int = 0) -> dict:
    key_of = jax.random.split(jax.random.key(seed), 13)
    part_keys = jax.random.split(jax.random.fold_in(key_of[12], part), 13)
    ssm_input = centred(part_keys[0], (SEQ, SSM_HEADS * HEAD_P), 1.0, 6.0, ((0, 16),))
    gate_input = centred(part_keys[1], (SEQ, SSM_HEADS * HEAD_P), 1.0, 6.0, ((0, 16),))
    b_proj = centred(part_keys[2], (SEQ, GROUPS * STATE), 0.03, 0.1796875, ((0, 16),))
    c_proj = centred(part_keys[3], (SEQ, GROUPS * STATE), 1.0, 6.0, ((0, 16),))
    dt_raw = draw_dt_raw(jax.random.fold_in(jax.random.fold_in(key_of[12], part), 71), part)
    a_log = draw_a_log(jax.random.fold_in(key_of[12], 71), part)
    skip = jnp.clip(jax.random.uniform(key_of[6], (SSM_HEADS,), jnp.float32, 1.0, 3.0), 1.0, 3.0)
    norm_gain = jnp.clip(1.0 + 0.1 * jax.random.normal(key_of[7], (SSM_HEADS * HEAD_P,), jnp.float32), 0.5, 1.5)
    queries = draw_queries(jax.random.fold_in(jax.random.fold_in(key_of[12], part), 71), part)
    keys = draw_keys(jax.random.fold_in(jax.random.fold_in(key_of[12], part), 71), part)
    values = centred(part_keys[10], (SEQ, KVHEADS * HEAD_D), 1.0, 6.0, ((0, 16),))
    block_lists = draw_block_lists(jax.random.fold_in(jax.random.fold_in(key_of[12], part), 71), part)
    return dict(ssm_input=ssm_input, gate_input=gate_input, b_proj=b_proj, c_proj=c_proj, dt_raw=dt_raw, a_log=a_log, skip=skip, norm_gain=norm_gain, queries=queries, keys=keys, values=values, block_lists=block_lists)


NORM_EPS = 1e-05

def block_terms(inputs_blk, steps_blk, b_blk, c_blk, head_rates):
    running = jnp.cumsum(-steps_blk * head_rates, axis=0)
    scaled = lax.optimization_barrier((inputs_blk.astype(jnp.float32) * steps_blk[..., None]).astype(jnp.bfloat16))
    products = jnp.einsum('tgn,sgn->gts', c_blk.astype(jnp.float32), b_blk.astype(jnp.float32))
    ordered = jnp.transpose(running, (1, 2, 0))
    spacing = ordered[..., :, None] - ordered[..., None, :]
    length = running.shape[0]
    lower_tri = jnp.arange(length)[:, None] >= jnp.arange(length)[None, :]
    decays = jnp.where(lower_tri, jnp.exp(jnp.where(lower_tri, spacing, 0.0)), 0.0)
    mixing = lax.optimization_barrier((decays * products[:, None]).astype(jnp.bfloat16))
    diag_out = jnp.einsum('gjts,sgjp->tgjp', mixing.astype(jnp.float32), scaled.astype(jnp.float32))
    tail_decay = jnp.exp(running[-1] - running)
    b_decay = lax.optimization_barrier((b_blk.astype(jnp.float32)[:, :, None, :] * tail_decay[..., None]).astype(jnp.bfloat16))
    span_state = jnp.einsum('sgjp,sgjn->gjpn', scaled.astype(jnp.float32), b_decay.astype(jnp.float32))
    return (diag_out, span_state, running)

def state_terms(c_blk, running, state):
    rounded = lax.optimization_barrier(state.astype(jnp.bfloat16))
    from_state = jnp.einsum('tgn,gjpn->tgjp', c_blk.astype(jnp.float32), rounded.astype(jnp.float32))
    return jnp.exp(running)[..., None] * from_state

def finish(mixed, ssm_input, gate_input, skip, norm_gain):
    layout = mixed.shape
    with_skip = mixed + skip.reshape(layout[1], layout[2], 1) * ssm_input.reshape(layout).astype(jnp.float32)
    gated = with_skip * jax.nn.silu(gate_input.astype(jnp.float32)).reshape(layout)
    grouped = gated.reshape(layout[0], layout[1], layout[2] * layout[3])
    scale_rms = lax.rsqrt(lax.optimization_barrier(jnp.mean(grouped * grouped, axis=-1, keepdims=True)) + NORM_EPS)
    normed = grouped * scale_rms * norm_gain.reshape(1, layout[1], -1)
    return normed.reshape(layout[0], -1).astype(jnp.bfloat16)

def reference(ssm_input, gate_input, b_proj, c_proj, dt_raw, a_log, skip, norm_gain, queries, keys, values, block_lists):
    per_group = SSM_HEADS // GROUPS
    blocks = SEQ // BLK
    inputs_all = ssm_input.reshape(blocks, BLK, GROUPS, per_group, HEAD_P)
    steps_all = jax.nn.softplus(dt_raw).reshape(blocks, BLK, GROUPS, per_group)
    b_all = b_proj.reshape(blocks, BLK, GROUPS, STATE)
    c_all = c_proj.reshape(blocks, BLK, GROUPS, STATE)
    head_rates = jnp.exp(a_log).reshape(GROUPS, per_group)

    def advance(state, pieces):
        inputs_blk, steps_blk, b_blk, c_blk = pieces
        diag_out, span_state, running = block_terms(inputs_blk, steps_blk, b_blk, c_blk, head_rates)
        outputs = diag_out + state_terms(c_blk, running, state)
        state = jnp.exp(running[-1])[..., None, None] * state + span_state
        return (state, outputs)
    start_state = jnp.zeros((GROUPS, per_group, HEAD_P, STATE), jnp.float32)
    _, mixed = lax.scan(advance, start_state, (inputs_all, steps_all, b_all, c_all))
    ssm_out = finish(mixed.reshape(SEQ, GROUPS, per_group, HEAD_P), ssm_input, gate_input, skip, norm_gain)
    ratio_heads = QHEADS // KVHEADS
    query_blocks = queries.reshape(blocks, BLK, KVHEADS, ratio_heads, HEAD_D)
    key_heads = keys.reshape(SEQ, KVHEADS, HEAD_D).astype(jnp.float32)
    value_heads = values.reshape(SEQ, KVHEADS, HEAD_D).astype(jnp.float32)
    key_pos = jnp.arange(SEQ)
    key_block = key_pos // BLK
    scale_score = HEAD_D ** (-0.5)

    def attend(pieces):
        query_blk, listed, block_index = pieces
        listed_key = jnp.any(listed[:, None] == key_block[None, :], axis=0)
        query_pos = block_index * BLK + jnp.arange(BLK)
        visible = listed_key[None, :] | (key_block[None, :] == block_index) & (key_pos[None, :] <= query_pos[:, None])
        scores = jnp.einsum('tkgd,skd->kgts', query_blk.astype(jnp.float32), key_heads) * scale_score
        scores = jnp.where(visible, scores, -jnp.inf)
        weight = jnp.exp(scores - lax.optimization_barrier(jnp.max(scores, axis=-1, keepdims=True)))
        weight_sum = lax.optimization_barrier(jnp.sum(weight, axis=-1))
        rounded = lax.optimization_barrier(weight.astype(jnp.bfloat16))
        summed = jnp.einsum('kgts,skd->tkgd', rounded.astype(jnp.float32), value_heads)
        result = summed / jnp.transpose(weight_sum, (2, 0, 1))[..., None]
        return result.reshape(BLK, QHEADS * HEAD_D).astype(jnp.bfloat16)
    attn_out = lax.map(attend, (query_blocks, block_lists, jnp.arange(blocks)))
    return (ssm_out, attn_out.reshape(SEQ, QHEADS * HEAD_D))
```

```python
import jax
import jax.numpy as jnp
from jax import lax
from jax.experimental import pallas as pl
from jax.experimental.pallas import tpu as pltpu
from jax.sharding import PartitionSpec as P

MESH = pl.DeviceIdType.MESH
F32 = jnp.float32
BF16 = jnp.bfloat16

SSM_HEADS = 64
HEAD_P = 64
GROUPS = 4
KVHEADS = 4
RATIO = 4
HEAD_D = 128
BLK = 128
NORM_EPS = 1e-05
MASKED = -1e30

CHIPS = 8
HALF = 512
COLS = 1024
PIECE = 128
CHUNKS = 16
UP_STEPS = 3
DOWN_STEPS = 4
LAG_NUM, LAG_DEN = 9, 2
KV_TICKS = 4
ATTN_LAST = 34
ATTN_FIRST = 26
TICKS = 64


def dot(a, b):
    return lax.dot_general(a, b, (((1,), (0,)), ((), ())), preferred_element_type=F32)


def dot_t(a, b):
    return lax.dot_general(a, b, (((1,), (1,)), ((), ())), preferred_element_type=F32)


def split(v):
    hi = v.astype(BF16)
    return hi, (v - hi.astype(F32)).astype(BF16)


def kernel(
    x_hbm, gate_hbm, b_hbm, c_hbm, dt_hbm, alog_hbm, skip_hbm, gain_hbm, q_hbm, k_hbm, v_hbm, list_hbm,
    ssm_hbm, attn_hbm,
    x, gate, b, cp, dtr, alog, skip, gain, q, lists,
    kv, stack, xs, u, a1, a2, local, sib, dec, dsib, chip, isend, pin, enter, ssm_v, attn_v,
    in_sem, out_sem,
    up_s, up_r, down_s, down_r, kvsib_s, kvsib_r, chain_s, chain_r, psib_s, psib_r, ex_s, ex_r,
):
    me = lax.axis_index("ctx")
    y = lax.div(me, 2)
    c = lax.rem(me, 2)
    oc = 1 - c
    above = lax.rem(y + 1, CHIPS) * 2 + c
    below = lax.rem(y + CHIPS - 1, CHIPS) * 2 + c
    other = y * 2 + oc

    barrier = pltpu.get_barrier_semaphore()
    for peer in (above, below, other):
        pl.semaphore_signal(barrier, inc=1, device_id={"ctx": peer}, device_id_type=MESH)

    loads = [
        pltpu.make_async_copy(src, dst, in_sem.at[i])
        for i, (src, dst) in enumerate(
            (
                (dt_hbm, dtr), (alog_hbm, alog), (skip_hbm, skip), (b_hbm, b), (x_hbm, x),
                (k_hbm, kv.at[me, 0]), (v_hbm, kv.at[me, 1]), (c_hbm, cp), (gate_hbm, gate), (gain_hbm, gain),
                (q_hbm, q), (list_hbm, lists),
            )
        )
    ]
    for load in loads:
        load.start()

    def remote(src, dst, send, recv, to):
        return pltpu.make_async_remote_copy(
            src_ref=src, dst_ref=dst, send_sem=send, recv_sem=recv, device_id={"ctx": to}, device_id_type=MESH
        )

    def up_copy(e):
        slot = lax.rem(y - lax.div(e, 2) + CHIPS, CHIPS) * 2 + c
        part = lax.rem(e, 2)
        return remote(kv.at[slot, part], kv.at[slot, part], up_s.at[e], up_r.at[e], above)

    def up_arrival(e):
        slot = lax.rem(y - 1 - lax.div(e, 2) + CHIPS, CHIPS) * 2 + c
        part = lax.rem(e, 2)
        return remote(kv.at[slot, part], kv.at[slot, part], up_s.at[e], up_r.at[e], above), slot, part

    def down_copy(e):
        slot = lax.rem(y + lax.div(e, 2), CHIPS) * 2 + c
        part = lax.rem(e, 2)
        return remote(kv.at[slot, part], kv.at[slot, part], down_s.at[e], down_r.at[e], below)

    def down_arrival(e):
        slot = lax.rem(y + 1 + lax.div(e, 2), CHIPS) * 2 + c
        part = lax.rem(e, 2)
        return remote(kv.at[slot, part], kv.at[slot, part], down_s.at[e], down_r.at[e], below), slot, part

    def up_sends(e):
        return (y < CHIPS - 1) & (y - lax.div(e, 2) >= 0)

    def up_gets(e):
        return y - 1 - lax.div(e, 2) >= 0

    def down_sends(e):
        return lax.rem(y + lax.div(e, 2), CHIPS) < CHIPS - DOWN_STEPS

    def down_gets(e):
        return lax.rem(y + 1 + lax.div(e, 2), CHIPS) < CHIPS - DOWN_STEPS

    def down_keeps(e):
        return (y + 1 + lax.div(e, 2) >= CHIPS) & down_gets(e)

    def kv_sib(i, slot, part):
        return remote(kv.at[slot, part], kv.at[slot, part], kvsib_s.at[i], kvsib_r.at[i], other)

    UP0, DOWN0 = 2, 2 + 2 * UP_STEPS

    for load in loads[:3]:
        load.wait()
    raw = dtr[...]
    dt = jnp.maximum(raw, 0.0) + jnp.log1p(jnp.exp(-jnp.abs(raw)))
    rate = jnp.exp(alog[...])
    row = lax.broadcasted_iota(jnp.int32, (BLK, BLK), 0)
    col = lax.broadcasted_iota(jnp.int32, (BLK, BLK), 1)
    tri = row >= col
    cum = lax.dot_general(
        tri.astype(F32), -dt * rate, (((1,), (0,)), ((), ())), precision=lax.Precision.HIGHEST,
        preferred_element_type=F32,
    )
    w_hi, w_lo = split(dt * jnp.exp(-cum))
    u_hi, u_lo = split(jnp.exp(cum))
    s_hi, s_lo = split(jnp.broadcast_to(skip[...], (16, SSM_HEADS)))
    for i, part in enumerate((w_hi, w_lo, u_hi, u_lo)):
        stack[pl.ds(i * BLK, BLK), :] = part
    stack[pl.ds(4 * BLK, 16), :] = s_hi
    stack[pl.ds(4 * BLK + 16, 16), :] = s_lo
    for load in loads[3:5]:
        load.wait()

    def expansion(j):
        heads = HALF // HEAD_P
        r = lax.broadcasted_iota(jnp.int32, (SSM_HEADS, HALF), 0)
        k = lax.broadcasted_iota(jnp.int32, (SSM_HEADS, HALF), 1)
        return (r - j * heads == lax.shift_right_logical(k, 6)).astype(F32).astype(BF16)

    def own_state(j, carry):
        g, half = lax.div(j, 2), lax.rem(j, 2)
        cols = pl.ds(pl.multiple_of(j * HALF, HALF), HALF)
        wide = dot(stack[pl.ds(0, 4 * BLK), :], expansion(j))
        w = wide[0:BLK] + wide[BLK : 2 * BLK]
        uu = wide[2 * BLK : 3 * BLK] + wide[3 * BLK : 4 * BLK]
        scaled = (x[:, cols].astype(F32) * w).astype(BF16)
        xs[:, cols] = scaled
        u[:, cols] = uu
        last = uu[BLK - 1 : BLK, :]
        bt = jnp.transpose(b[:, pl.ds(pl.multiple_of(g * BLK, BLK), BLK)].astype(F32)).astype(BF16)
        state = dot(bt, scaled) * last
        for i in range(4):
            piece = slice(i * PIECE, (i + 1) * PIECE)
            local[half, g * 4 + i] = state[:, piece].astype(BF16)
            dec[half, g * 4 + i] = jnp.broadcast_to(last[:, piece], (8, PIECE))
        return carry

    lax.fori_loop(0, 2 * GROUPS, own_state, 0)

    for load in loads[5:7]:
        load.wait()
    pl.semaphore_wait(barrier, 3)

    ex_d = remote(dec, dsib, ex_s.at[0], ex_r.at[0], other)
    ex_chain = remote(local.at[oc], sib.at[oc], ex_s.at[1], ex_r.at[1], other)
    ex_chain_in = remote(local.at[c], sib.at[c], ex_s.at[1], ex_r.at[1], other)
    ex_rest = remote(local.at[0], sib.at[0], ex_s.at[2], ex_r.at[2], other)
    ex_d.start()
    ex_chain.start()

    for e in range(2):
        @pl.when(down_sends(e))
        def _(e=e):
            down_copy(e).start()

        @pl.when(up_sends(e))
        def _(e=e):
            up_copy(e).start()

    @pl.when(c == 0)
    def _():
        ex_rest.start()

    for e in range(2):
        kv_sib(e, me, e).start()

    ex_d.wait()
    ex_chain.wait_send()
    ex_chain_in.wait_recv()
    first = (c == 0).astype(F32)

    def chip_state(k, carry):
        mine, theirs = local[c, k].astype(F32), sib[c, k].astype(F32)
        d_mine, d_theirs = dec[c, k][0:1, :], dsib[c, k][0:1, :]
        value = first * (d_theirs * mine + theirs) + (1.0 - first) * (d_mine * theirs + mine)
        chip[k] = value

        @pl.when(y == 0)
        def _():
            isend[k] = value.astype(BF16)
            pin[c, k] = jnp.zeros((BLK, PIECE), BF16)
            remote(isend.at[k], pin.at[c, k], chain_s.at[k], chain_r.at[k], above).start()
            remote(pin.at[c, k], pin.at[c, k], psib_s.at[k], psib_r.at[k], other).start()

        return carry

    lax.fori_loop(0, CHUNKS, chip_state, 0)

    for load in loads[7:]:
        load.wait()

    def own_part(j, carry):
        g = lax.div(j, 2)
        cols = pl.ds(pl.multiple_of(j * HALF, HALF), HALF)
        state_cols = pl.ds(pl.multiple_of(g * BLK, BLK), BLK)
        wide = dot(stack[pl.ds(4 * BLK, 32), :], expansion(j))
        sk = wide[0:1] + wide[16:17]
        products = dot_t(cp[:, state_cols], b[:, state_cols])
        mixing = jnp.where(tri, products, 0.0).astype(BF16)
        uu = u[:, cols]
        base = uu * dot(mixing, xs[:, cols]) + sk * x[:, cols].astype(F32)
        gt = gate[:, cols].astype(F32)
        act = gt / (1.0 + jnp.exp(-gt))
        a1[:, cols] = base * act
        a2[:, cols] = uu * act
        return carry

    lax.fori_loop(0, 2 * GROUPS, own_part, 0)

    def attention(kh):
        blocks = [lists[0, i] for i in range(3)]
        slots = [jnp.where(i < 0, me, i) for i in blocks]
        biases = [jnp.where(i < 0, MASKED, 0.0).astype(F32) for i in blocks]
        cols = pl.ds(pl.multiple_of(kh * HEAD_D, HEAD_D), HEAD_D)
        queries = jnp.concatenate(
            [q[:, pl.ds(pl.multiple_of((kh * RATIO + i) * HEAD_D, HEAD_D), HEAD_D)] for i in range(RATIO)], axis=0
        )
        scale = HEAD_D ** (-0.5)
        tri4 = jnp.concatenate([tri] * RATIO, axis=0)
        scores = [jnp.where(tri4, dot_t(queries, kv[me, 0, :, cols]) * scale, MASKED)]
        for slot, bias in zip(slots, biases):
            scores.append(dot_t(queries, kv[slot, 0, :, cols]) * scale + bias)
        top = scores[0]
        for s in scores[1:]:
            top = jnp.maximum(top, s)
        top = jnp.max(top, axis=1, keepdims=True)
        weights = [jnp.exp(s - top) for s in scores]
        total = weights[0] + weights[1] + weights[2] + weights[3]
        total = jnp.sum(total, axis=1, keepdims=True)
        acc = dot(weights[0].astype(BF16), kv[me, 1, :, cols])
        for slot, weight in zip(slots, weights[1:]):
            acc = acc + dot(weight.astype(BF16), kv[slot, 1, :, cols])
        out = (acc / total).astype(BF16)
        for i in range(RATIO):
            attn_v[:, pl.ds(pl.multiple_of((kh * RATIO + i) * HEAD_D, HEAD_D), HEAD_D)] = out[i * BLK : (i + 1) * BLK]

    reach = lax.div(y * LAG_NUM, LAG_DEN)
    attn_at = jnp.where(y == CHIPS - 1, ATTN_LAST, jnp.maximum(reach + CHUNKS + 1, ATTN_FIRST))

    def tick(t, carry):
        k = t - reach

        @pl.when((y > 0) & (k >= 0) & (k < CHUNKS))
        def _():
            into = remote(isend.at[k], pin.at[c, k], chain_s.at[k], chain_r.at[k], above)
            into.wait_recv()

            @pl.when(y < CHIPS - 1)
            def _():
                d = dec[c, k][0:1, :] * dsib[c, k][0:1, :]
                isend[k] = (d * pin[c, k].astype(F32) + chip[k]).astype(BF16)
                into.start()

            remote(pin.at[c, k], pin.at[c, k], psib_s.at[k], psib_r.at[k], other).start()

        e = lax.div(t, KV_TICKS) - 1
        now = (lax.rem(t, KV_TICKS) == 0) & (e >= 0)

        @pl.when(now & (e < 2 * DOWN_STEPS) & down_gets(jnp.maximum(e, 0)))
        def _():
            arrival, slot, part = down_arrival(e)
            arrival.wait_recv()

            @pl.when(e < 2 * DOWN_STEPS - 2)
            def _():
                down_copy(e + 2).start()

            @pl.when(down_keeps(e))
            def _():
                kv_sib(DOWN0 + e, slot, part).start()

        @pl.when(now & (e < 2 * UP_STEPS) & up_gets(jnp.maximum(e, 0)))
        def _():
            arrival, slot, part = up_arrival(e)
            arrival.wait_recv()

            @pl.when((e < 2 * UP_STEPS - 2) & (y < CHIPS - 1))
            def _():
                up_copy(e + 2).start()

            kv_sib(UP0 + e, slot, part).start()

        @pl.when(t == attn_at)
        def _():
            def wait_sib(i, carry):
                kv_sib(i, me, 0).wait_recv()
                return carry

            lax.fori_loop(0, 2, wait_sib, 0)

            def wait_up(i, carry):
                @pl.when(up_gets(i))
                def _():
                    kv_sib(UP0 + i, me, 0).wait_recv()
                return carry

            def wait_down(i, carry):
                @pl.when(down_keeps(i))
                def _():
                    kv_sib(DOWN0 + i, me, 0).wait_recv()
                return carry

            lax.fori_loop(0, 2 * UP_STEPS, wait_up, 0)
            lax.fori_loop(0, 2 * DOWN_STEPS, wait_down, 0)

        @pl.when((t >= attn_at) & (t < attn_at + KVHEADS))
        def _():
            attention(t - attn_at)

        return carry

    lax.fori_loop(0, TICKS, tick, 0)
    attn_out = pltpu.make_async_copy(attn_v, attn_hbm, out_sem.at[0])
    attn_out.start()

    @pl.when(c == 1)
    def _():
        ex_rest.wait_recv()

    def finish(g, carry):
        cols = pl.ds(pl.multiple_of(g * COLS, COLS), COLS)
        state_cols = pl.ds(pl.multiple_of(g * BLK, BLK), BLK)
        for i in range(4):
            k = g * 4 + i
            remote(pin.at[oc, k], pin.at[oc, k], psib_s.at[k], psib_r.at[k], other).wait_recv()
        for half in range(2):
            for i in range(4):
                k = g * 4 + i

                @pl.when(c == 0)
                def _(half=half, i=i, k=k):
                    enter[:, (half * 4 + i) * PIECE : (half * 4 + i + 1) * PIECE] = pin[half, k]

                @pl.when(c == 1)
                def _(half=half, i=i, k=k):
                    came = dsib[half, k][0:1, :] * pin[half, k].astype(F32) + sib[half, k].astype(F32)
                    enter[:, (half * 4 + i) * PIECE : (half * 4 + i + 1) * PIECE] = came.astype(BF16)

        gated = a1[:, cols] + a2[:, cols] * dot(cp[:, state_cols], enter[...])
        square = jnp.sum(gated * gated, axis=1, keepdims=True)
        scale = lax.rsqrt(square * (1.0 / COLS) + NORM_EPS)
        ssm_v[:, cols] = (gated * scale * gain[:, cols]).astype(BF16)
        return carry

    lax.fori_loop(0, GROUPS, finish, 0)
    ssm_out = pltpu.make_async_copy(ssm_v, ssm_hbm, out_sem.at[1])
    ssm_out.start()

    @pl.when(c == 0)
    def _():
        ex_rest.wait_send()

    def wait_chain(k, carry):
        remote(pin.at[c, k], pin.at[c, k], psib_s.at[k], psib_r.at[k], other).wait_send()

        @pl.when(y < CHIPS - 1)
        def _():
            remote(isend.at[k], pin.at[c, k], chain_s.at[k], chain_r.at[k], above).wait_send()
        return carry

    lax.fori_loop(0, CHUNKS, wait_chain, 0)

    def wait_up_sent(e, carry):
        @pl.when(up_sends(e))
        def _():
            up_copy(e).wait_send()

        @pl.when(up_gets(e))
        def _():
            kv_sib(UP0 + e, me, 0).wait_send()
        return carry

    def wait_down_sent(e, carry):
        @pl.when(down_sends(e))
        def _():
            down_copy(e).wait_send()

        @pl.when(down_keeps(e))
        def _():
            kv_sib(DOWN0 + e, me, 0).wait_send()
        return carry

    lax.fori_loop(0, 2 * UP_STEPS, wait_up_sent, 0)
    lax.fori_loop(0, 2 * DOWN_STEPS, wait_down_sent, 0)
    for e in range(2):
        kv_sib(e, me, e).wait_send()
    attn_out.wait()
    ssm_out.wait()


def body(ssm_input, gate_input, b_proj, c_proj, dt_raw, a_log, skip, norm_gain, queries, keys, values, block_lists):
    vmem = pltpu.VMEM
    dma = lambda n: pltpu.SemaphoreType.DMA((n,))
    wide = GROUPS * COLS
    any_spec = pl.BlockSpec(memory_space=pl.ANY)
    return pl.pallas_call(
        kernel,
        out_shape=(
            jax.ShapeDtypeStruct((BLK, wide), BF16),
            jax.ShapeDtypeStruct((BLK, KVHEADS * RATIO * HEAD_D), BF16),
        ),
        in_specs=[any_spec] * 12,
        out_specs=(any_spec, any_spec),
        scratch_shapes=[
            vmem((BLK, wide), BF16), vmem((BLK, wide), BF16), vmem((BLK, GROUPS * BLK), BF16),
            vmem((BLK, GROUPS * BLK), BF16), vmem((BLK, SSM_HEADS), F32), vmem((1, SSM_HEADS), F32),
            vmem((1, SSM_HEADS), F32), vmem((1, wide), F32), vmem((BLK, KVHEADS * RATIO * HEAD_D), BF16),
            pltpu.SMEM((1, 3), jnp.int32),
            vmem((2 * CHIPS, 2, BLK, KVHEADS * HEAD_D), BF16),
            vmem((4 * BLK + 32, SSM_HEADS), BF16),
            vmem((BLK, wide), BF16), vmem((BLK, wide), F32), vmem((BLK, wide), F32), vmem((BLK, wide), F32),
            vmem((2, CHUNKS, BLK, PIECE), BF16), vmem((2, CHUNKS, BLK, PIECE), BF16),
            vmem((2, CHUNKS, 8, PIECE), F32), vmem((2, CHUNKS, 8, PIECE), F32),
            vmem((CHUNKS, BLK, PIECE), F32), vmem((CHUNKS, BLK, PIECE), BF16),
            vmem((2, CHUNKS, BLK, PIECE), BF16), vmem((BLK, COLS), BF16),
            vmem((BLK, wide), BF16), vmem((BLK, KVHEADS * RATIO * HEAD_D), BF16),
            dma(12), dma(2),
            dma(2 * UP_STEPS), dma(2 * UP_STEPS), dma(2 * DOWN_STEPS), dma(2 * DOWN_STEPS),
            dma(2 + 2 * UP_STEPS + 2 * DOWN_STEPS), dma(2 + 2 * UP_STEPS + 2 * DOWN_STEPS),
            dma(CHUNKS), dma(CHUNKS), dma(CHUNKS), dma(CHUNKS), dma(3), dma(3),
        ],
        compiler_params=pltpu.CompilerParams(
            collective_id=0, has_side_effects=True, vmem_limit_bytes=48 * 2**20
        ),
        name="layers",
    )(
        ssm_input, gate_input, b_proj, c_proj, dt_raw, a_log.reshape(1, -1), skip.reshape(1, -1),
        norm_gain.reshape(1, -1), queries, keys, values, block_lists,
    )


def solution(mesh):
    rows = P(("dp", "ctx"), None)
    in_specs = (rows, rows, rows, rows, rows, P(), P(), P(), rows, rows, rows, rows)
    return jax.shard_map(body, mesh=mesh, in_specs=in_specs, out_specs=(rows, rows), check_vma=False)
```

```python
import jax
import jax.numpy as jnp
from jax import lax
from jax.experimental import pallas as pl
from jax.experimental.pallas import tpu as pltpu
from jax.sharding import PartitionSpec as P

MESH = pl.DeviceIdType.MESH
F32 = jnp.float32
BF16 = jnp.bfloat16

SSM_HEADS = 64
HEAD_P = 64
GROUPS = 4
KVHEADS = 4
RATIO = 4
HEAD_D = 128
BLK = 128
NORM_EPS = 1e-05
MASKED = -1e30

CHIPS = 8
HALF = 512
COLS = 1024
PIECE = 128
PER_GROUP = 4
CHUNKS = GROUPS * PER_GROUP
UP_STEPS = 3
DOWN_STEPS = 5
LAG_NUM, LAG_DEN = 9, 2
KV_TICKS = 4
ATTN_TICK = (26, 22, 31, 41, 41, 41, 33, 33)
ATTN_HEADS = 2
STORES = 2
ATTN_PIECES = KVHEADS * RATIO // ATTN_HEADS


def dot(a, b):
    return lax.dot_general(a, b, (((1,), (0,)), ((), ())), preferred_element_type=F32)


def dot_t(a, b):
    return lax.dot_general(a, b, (((1,), (1,)), ((), ())), preferred_element_type=F32)


def split(v):
    hi = v.astype(BF16)
    return hi, (v - hi.astype(F32)).astype(BF16)


def pick(y, table):
    value = table[0]
    for i in range(1, CHIPS):
        value = jnp.where(y == i, table[i], value)
    return value


def kernel(
    x_hbm, gate_hbm, b_hbm, c_hbm, dt_hbm, alog_hbm, skip_hbm, gain_hbm, q_hbm, k_hbm, v_hbm, list_hbm,
    ssm_hbm, attn_hbm,
    x, gate, b, cp, dtr, alog, skip, gain, q, lists,
    kv, stack, spread, bt, xs, a1, a2, local, sib, dec, dsib, chip, isend, pin, enter, ssm_v, attn_v,
    in_sem, out_sem,
    up_s, up_r, down_s, down_r, kvsib_s, kvsib_r, chain_s, chain_r, psib_s, psib_r, ex_s, ex_r,
):
    me = lax.axis_index("ctx")
    y = lax.div(me, 2)
    c = lax.rem(me, 2)
    oc = 1 - c
    above = lax.rem(y + 1, CHIPS) * 2 + c
    below = lax.rem(y + CHIPS - 1, CHIPS) * 2 + c
    other = y * 2 + oc

    barrier = pltpu.get_barrier_semaphore()
    for peer in (above, below, other):
        pl.semaphore_signal(barrier, inc=1, device_id={"ctx": peer}, device_id_type=MESH)

    loads = [
        pltpu.make_async_copy(src, dst, in_sem.at[i])
        for i, (src, dst) in enumerate(
            (
                (dt_hbm, dtr), (alog_hbm, alog), (skip_hbm, skip), (b_hbm, b),
                (k_hbm, kv.at[me, 0]), (v_hbm, kv.at[me, 1]), (x_hbm, x), (c_hbm, cp), (gate_hbm, gate),
                (gain_hbm, gain), (q_hbm, q), (list_hbm, lists),
            )
        )
    ]
    for load in loads:
        load.start()

    def remote(src, dst, send, recv, to):
        return pltpu.make_async_remote_copy(
            src_ref=src, dst_ref=dst, send_sem=send, recv_sem=recv, device_id={"ctx": to}, device_id_type=MESH
        )

    def up_copy(e, ahead=0):
        slot = lax.rem(y - ahead - lax.div(e, 2) + CHIPS, CHIPS) * 2 + c
        part = lax.rem(e, 2)
        return remote(kv.at[slot, part], kv.at[slot, part], up_s.at[e], up_r.at[e], above), slot, part

    def down_copy(e, ahead=0):
        slot = lax.rem(y + ahead + lax.div(e, 2), CHIPS) * 2 + c
        part = lax.rem(e, 2)
        return remote(kv.at[slot, part], kv.at[slot, part], down_s.at[e], down_r.at[e], below), slot, part

    def up_sends(e):
        step = lax.div(e, 2)
        return (y < CHIPS - 1) & (y >= step) & ((step < 2) | (y - step >= 3))

    def up_gets(e):
        step = lax.div(e, 2)
        return (y >= 1 + step) & ((step < 2) | (y - 1 - step >= 3))

    def down_goes(source, step):
        return (source < 3) | ((source == 3) & (step < 4))

    def down_sends(e):
        step = lax.div(e, 2)
        return down_goes(lax.rem(y + step, CHIPS), step)

    def down_gets(e):
        step = lax.div(e, 2)
        return down_goes(lax.rem(y + 1 + step, CHIPS), step)

    def down_keeps(e):
        return (y + 1 + lax.div(e, 2) >= CHIPS) & down_gets(e)

    def kv_sib(i, slot, part):
        return remote(kv.at[slot, part], kv.at[slot, part], kvsib_s.at[i], kvsib_r.at[i], other)

    UP0, DOWN0 = 2, 2 + 2 * UP_STEPS

    r = lax.broadcasted_iota(jnp.int32, (SSM_HEADS, HALF), 0)
    h = lax.shift_right_logical(lax.broadcasted_iota(jnp.int32, (SSM_HEADS, HALF), 1), 6)
    for j in range(2 * GROUPS):
        spread[j] = (r - j * (HALF // HEAD_P) == h).astype(F32).astype(BF16)

    for load in loads[:4]:
        load.wait()
    raw = jnp.transpose(dtr[...])
    dt = jnp.maximum(raw, 0.0) + jnp.log1p(jnp.exp(-jnp.abs(raw)))
    rate = jnp.exp(alog[...])
    row = lax.broadcasted_iota(jnp.int32, (BLK, BLK), 0)
    col = lax.broadcasted_iota(jnp.int32, (BLK, BLK), 1)
    tri = row >= col
    cum = lax.dot_general(
        tri.astype(F32), -dt * rate, (((1,), (0,)), ((), ())), precision=lax.Precision.HIGHEST,
        preferred_element_type=F32,
    )
    up_to = jnp.exp(cum)
    l_hi, l_lo = split(jnp.broadcast_to(up_to[BLK - 1 : BLK], (16, SSM_HEADS)))
    s_hi, s_lo = split(jnp.broadcast_to(skip[...], (16, SSM_HEADS)))
    stack[0:BLK, :] = (dt * jnp.exp(-cum)).astype(BF16)
    stack[BLK : BLK + 16, :] = l_hi
    stack[BLK + 16 : BLK + 32, :] = l_lo
    stack[BLK + 32 : 2 * BLK + 32, :] = up_to.astype(BF16)
    stack[2 * BLK + 32 : 2 * BLK + 48, :] = s_hi
    stack[2 * BLK + 48 : 2 * BLK + 64, :] = s_lo
    for g in range(GROUPS):
        bt[g] = jnp.transpose(b[:, g * BLK : (g + 1) * BLK].astype(F32)).astype(BF16)
    for load in loads[4:7]:
        load.wait()

    pl.semaphore_wait(barrier, 3)
    for e in range(2):
        @pl.when(down_sends(e))
        def _(e=e):
            down_copy(e)[0].start()

        @pl.when(up_sends(e))
        def _(e=e):
            up_copy(e)[0].start()

    def ex_d(g):
        some = pl.ds(g * PER_GROUP, PER_GROUP)
        return remote(dec.at[some], dsib.at[some], ex_s.at[g], ex_r.at[g], other)

    def ex_half(g, half):
        some = pl.ds(g * PER_GROUP, PER_GROUP)
        i = GROUPS + g
        return remote(local.at[half, some], sib.at[half, some], ex_s.at[i], ex_r.at[i], other)

    ex_rest = remote(local.at[0], sib.at[0], ex_s.at[2 * GROUPS], ex_r.at[2 * GROUPS], other)
    first = (c == 0).astype(F32)

    def own_state(g):
        for half in range(2):
            j = 2 * g + half
            cols = pl.ds(j * HALF, HALF)
            wide = dot(stack[0 : BLK + 32, :], spread[j])
            scaled = (x[:, cols].astype(F32) * wide[0:BLK]).astype(BF16)
            xs[:, cols] = scaled
            last = wide[BLK : BLK + 1] + wide[BLK + 16 : BLK + 17]
            state = dot(bt[g], scaled) * last
            for i in range(PER_GROUP):
                piece = slice(i * PIECE, (i + 1) * PIECE)
                local[half, g * PER_GROUP + i] = state[:, piece].astype(BF16)
                dec[g * PER_GROUP + i, half] = jnp.broadcast_to(last[:, piece], (8, PIECE))

    def chip_state(g):
        ex_d(g).wait_recv()
        ex_half(g, c).wait_recv()

        def one(i, carry):
            k = g * PER_GROUP + i
            mine, theirs = local[c, k].astype(F32), sib[c, k].astype(F32)
            d_mine, d_theirs = dec[k, c][0:1, :], dsib[k, c][0:1, :]
            value = first * (d_theirs * mine + theirs) + (1.0 - first) * (d_mine * theirs + mine)
            chip[k] = value

            @pl.when(y == 0)
            def _():
                isend[k] = value.astype(BF16)
                remote(isend.at[k], pin.at[c, k], chain_s.at[k], chain_r.at[k], above).start()
                pin[0, k] = jnp.zeros((BLK, PIECE), BF16)
                pin[1, k] = jnp.zeros((BLK, PIECE), BF16)

            return carry

        lax.fori_loop(0, PER_GROUP, one, 0)

    for g in range(GROUPS):
        own_state(g)
        ex_d(g).start()
        ex_half(g, oc).start()
        if g > 0:
            chip_state(g - 1)
    chip_state(GROUPS - 1)

    @pl.when(c == 0)
    def _():
        ex_rest.start()

    for e in range(2):
        kv_sib(e, me, e).start()

    for load in loads[7:]:
        load.wait()

    def own_part(j, carry):
        g = lax.div(j, 2)
        cols = pl.ds(pl.multiple_of(j * HALF, HALF), HALF)
        state_cols = pl.ds(pl.multiple_of(g * BLK, BLK), BLK)
        wide = dot(stack[BLK + 32 : 2 * BLK + 64, :], spread[j])
        uu = wide[0:BLK]
        sk = wide[BLK : BLK + 1] + wide[BLK + 16 : BLK + 17]
        products = dot_t(cp[:, state_cols], b[:, state_cols])
        mixing = jnp.where(tri, products, 0.0).astype(BF16)
        base = uu * dot(mixing, xs[:, cols]) + sk * x[:, cols].astype(F32)
        gt = gate[:, cols].astype(F32)
        act = gt / (1.0 + jnp.exp(-gt))
        a1[:, cols] = base * act
        a2[:, cols] = uu * act
        return carry

    lax.fori_loop(0, 2 * GROUPS, own_part, 0)

    def attention(piece):
        blocks = [lists[0, i] for i in range(3)]
        slots = [me] + [jnp.where(i < 0, me, i) for i in blocks]
        biases = [jnp.where(i < 0, MASKED, 0.0).astype(F32) for i in blocks]
        kh = lax.div(piece * ATTN_HEADS, RATIO)
        cols = pl.ds(pl.multiple_of(kh * HEAD_D, HEAD_D), HEAD_D)
        heads = [
            pl.ds(pl.multiple_of((piece * ATTN_HEADS + i) * HEAD_D, HEAD_D), HEAD_D) for i in range(ATTN_HEADS)
        ]
        queries = jnp.concatenate([q[:, head] for head in heads], axis=0)
        scale = HEAD_D ** (-0.5)
        tris = jnp.concatenate([tri] * ATTN_HEADS, axis=0)
        scores = [dot_t(queries, kv[slot, 0, :, cols]) * scale for slot in slots]
        scores = [jnp.where(tris, scores[0], MASKED)] + [s + bias for s, bias in zip(scores[1:], biases)]
        top = jnp.maximum(jnp.maximum(scores[0], scores[1]), jnp.maximum(scores[2], scores[3]))
        top = jnp.max(top, axis=1, keepdims=True)
        weights = [jnp.exp(s - top) for s in scores]
        total = (weights[0] + weights[1]) + (weights[2] + weights[3])
        total = jnp.sum(total, axis=1, keepdims=True)
        acc = dot(weights[0].astype(BF16), kv[slots[0], 1, :, cols])
        for slot, weight in zip(slots[1:], weights[1:]):
            acc = acc + dot(weight.astype(BF16), kv[slot, 1, :, cols])
        out = (acc / total).astype(BF16)
        for i, head in enumerate(heads):
            attn_v[:, head] = out[i * BLK : (i + 1) * BLK]

    def psib(half, k):
        return remote(pin.at[half, k], pin.at[half, k], psib_s.at[k], psib_r.at[k], other)

    def finish(g):
        @pl.when((c == 1) & (g == 0))
        def _():
            ex_rest.wait_recv()

        cols = pl.ds(pl.multiple_of(g * COLS, COLS), COLS)
        state_cols = pl.ds(pl.multiple_of(g * BLK, BLK), BLK)

        @pl.when(y > 0)
        def _():
            for i in range(PER_GROUP):
                psib(oc, g * PER_GROUP + i).wait_recv()

        for half in range(2):
            for i in range(PER_GROUP):
                k = g * PER_GROUP + i
                place = slice((half * PER_GROUP + i) * PIECE, (half * PER_GROUP + i + 1) * PIECE)

                @pl.when(c == 0)
                def _(half=half, k=k, place=place):
                    enter[:, place] = pin[half, k]

                @pl.when(c == 1)
                def _(half=half, k=k, place=place):
                    came = dsib[k, half][0:1, :] * pin[half, k].astype(F32) + sib[half, k].astype(F32)
                    enter[:, place] = came.astype(BF16)

        gated = a1[:, cols] + a2[:, cols] * dot(cp[:, state_cols], enter[...])
        square = jnp.sum(gated * gated, axis=1, keepdims=True)
        scale = lax.rsqrt(square * (1.0 / COLS) + NORM_EPS)
        ssm_v[:, cols] = (gated * scale * gain[:, cols]).astype(BF16)

    reach = lax.div(y * LAG_NUM, LAG_DEN)
    attn_at = pick(y, ATTN_TICK)
    end = jnp.maximum(reach + CHUNKS + 2, attn_at + ATTN_PIECES)
    late = (y == 1) | (y == 2)
    late_from = (y == 2) | (y == 3)

    def tick(t, carry):
        k = t - reach

        @pl.when((y > 0) & (k >= 0) & (k < CHUNKS))
        def _():
            into = remote(isend.at[k], pin.at[c, k], chain_s.at[k], chain_r.at[k], above)
            into.wait_recv()

            @pl.when(y < CHIPS - 1)
            def _():
                d = dec[k, c][0:1, :] * dsib[k, c][0:1, :]
                isend[k] = (d * pin[c, k].astype(F32) + chip[k]).astype(BF16)
                into.start()

            psib(c, k).start()

        @pl.when(late & (k == CHUNKS))
        def _():
            for e in (2, 3):
                up_copy(e)[0].start()

        @pl.when((k >= PER_GROUP + 1) & (lax.rem(k, PER_GROUP) == 1) & (k <= CHUNKS + 1))
        def _():
            finish(lax.div(k, PER_GROUP) - 1)

        e = lax.div(t, KV_TICKS) - 1
        now = (lax.rem(t, KV_TICKS) == 0) & (e >= 0)

        @pl.when(now & (e < 2 * DOWN_STEPS) & down_gets(jnp.maximum(e, 0)))
        def _():
            arrival, slot, part = down_copy(e, 1)
            arrival.wait_recv()

            @pl.when((e < 2 * DOWN_STEPS - 2) & down_sends(e + 2))
            def _():
                down_copy(e + 2)[0].start()

            @pl.when(down_keeps(e))
            def _():
                kv_sib(DOWN0 + e, slot, part).start()

        behind = late_from & (k >= CHUNKS + 1) & (k < CHUNKS + 3)
        u = jnp.where(behind, k - CHUNKS + 1, e)
        due = behind | (now & (e < 2 * UP_STEPS) & (jnp.logical_not(late_from) | (e < 2)))

        @pl.when(due & up_gets(jnp.maximum(u, 0)))
        def _():
            arrival, slot, part = up_copy(u, 1)
            arrival.wait_recv()

            @pl.when((u < 2 * UP_STEPS - 2) & up_sends(u + 2) & jnp.logical_not(late))
            def _():
                up_copy(u + 2)[0].start()

            kv_sib(UP0 + u, slot, part).start()

        @pl.when(t == attn_at)
        def _():
            for i in range(2):
                kv_sib(i, me, 0).wait_recv()

            def wait_up(i, carry):
                @pl.when(up_gets(i))
                def _():
                    kv_sib(UP0 + i, me, 0).wait_recv()
                return carry

            def wait_down(i, carry):
                @pl.when(down_keeps(i))
                def _():
                    kv_sib(DOWN0 + i, me, 0).wait_recv()
                return carry

            lax.fori_loop(0, 2 * UP_STEPS, wait_up, 0)
            lax.fori_loop(0, 2 * DOWN_STEPS, wait_down, 0)

        @pl.when((t >= attn_at) & (t < attn_at + ATTN_PIECES))
        def _():
            attention(t - attn_at)

        return carry

    lax.fori_loop(0, end, tick, 0)
    attn_out = pltpu.make_async_copy(attn_v, attn_hbm, out_sem.at[0])
    attn_out.start()
    ssm_out = pltpu.make_async_copy(ssm_v, ssm_hbm, out_sem.at[1])
    ssm_out.start()

    @pl.when(c == 0)
    def _():
        ex_rest.wait_send()

    for g in range(GROUPS):
        ex_d(g).wait_send()
        ex_half(g, oc).wait_send()

    def wait_chain(k, carry):
        @pl.when(y > 0)
        def _():
            psib(c, k).wait_send()

        @pl.when(y < CHIPS - 1)
        def _():
            remote(isend.at[k], pin.at[c, k], chain_s.at[k], chain_r.at[k], above).wait_send()
        return carry

    lax.fori_loop(0, CHUNKS, wait_chain, 0)

    def wait_up_sent(e, carry):
        @pl.when(up_sends(e))
        def _():
            up_copy(e)[0].wait_send()

        @pl.when(up_gets(e))
        def _():
            kv_sib(UP0 + e, me, 0).wait_send()
        return carry

    def wait_down_sent(e, carry):
        @pl.when(down_sends(e))
        def _():
            down_copy(e)[0].wait_send()

        @pl.when(down_keeps(e))
        def _():
            kv_sib(DOWN0 + e, me, 0).wait_send()
        return carry

    lax.fori_loop(0, 2 * UP_STEPS, wait_up_sent, 0)
    lax.fori_loop(0, 2 * DOWN_STEPS, wait_down_sent, 0)
    for e in range(2):
        kv_sib(e, me, e).wait_send()
    attn_out.wait()
    ssm_out.wait()


def store_kernel(ssm, attn, ssm_out, attn_out, ssm_v, attn_v, sem):
    parts = []
    for src, mid, dst in ((ssm, ssm_v, ssm_out), (attn, attn_v, attn_out)):
        for i in range(STORES):
            rows = pl.ds(i * (BLK // STORES), BLK // STORES)
            n = 2 * len(parts)
            parts.append(
                (
                    pltpu.make_async_copy(src.at[rows], mid.at[rows], sem.at[n]),
                    pltpu.make_async_copy(mid.at[rows], dst.at[rows], sem.at[n + 1]),
                )
            )
    for load, _ in parts:
        load.start()
    for load, store in parts:
        load.wait()
        store.start()
    for _, store in parts:
        store.wait()


def body(ssm_input, gate_input, b_proj, c_proj, dt_raw, a_log, skip, norm_gain, queries, keys, values, block_lists):
    vmem = pltpu.VMEM
    dma = lambda n: pltpu.SemaphoreType.DMA((n,))
    wide = GROUPS * COLS
    heads = KVHEADS * RATIO * HEAD_D
    any_spec = pl.BlockSpec(memory_space=pl.ANY)
    outs = (jax.ShapeDtypeStruct((BLK, wide), BF16), jax.ShapeDtypeStruct((BLK, heads), BF16))
    ssm, attn = pl.pallas_call(
        kernel,
        out_shape=outs,
        in_specs=[any_spec] * 12,
        out_specs=(any_spec, any_spec),
        scratch_shapes=[
            vmem((BLK, wide), BF16), vmem((BLK, wide), BF16), vmem((BLK, GROUPS * BLK), BF16),
            vmem((BLK, GROUPS * BLK), BF16), vmem((SSM_HEADS, BLK), F32), vmem((1, SSM_HEADS), F32),
            vmem((1, SSM_HEADS), F32), vmem((1, wide), F32), vmem((BLK, heads), BF16),
            pltpu.SMEM((1, 3), jnp.int32),
            vmem((2 * CHIPS, 2, BLK, KVHEADS * HEAD_D), BF16),
            vmem((2 * BLK + 64, SSM_HEADS), BF16), vmem((2 * GROUPS, SSM_HEADS, HALF), BF16),
            vmem((GROUPS, BLK, BLK), BF16),
            vmem((BLK, wide), BF16), vmem((BLK, wide), F32), vmem((BLK, wide), F32),
            vmem((2, CHUNKS, BLK, PIECE), BF16), vmem((2, CHUNKS, BLK, PIECE), BF16),
            vmem((CHUNKS, 2, 8, PIECE), F32), vmem((CHUNKS, 2, 8, PIECE), F32),
            vmem((CHUNKS, BLK, PIECE), F32), vmem((CHUNKS, BLK, PIECE), BF16),
            vmem((2, CHUNKS, BLK, PIECE), BF16), vmem((BLK, COLS), BF16),
            vmem((BLK, wide), BF16), vmem((BLK, heads), BF16),
            dma(12), dma(2),
            dma(2 * UP_STEPS), dma(2 * UP_STEPS), dma(2 * DOWN_STEPS), dma(2 * DOWN_STEPS),
            dma(2 + 2 * UP_STEPS + 2 * DOWN_STEPS), dma(2 + 2 * UP_STEPS + 2 * DOWN_STEPS),
            dma(CHUNKS), dma(CHUNKS), dma(CHUNKS), dma(CHUNKS), dma(2 * GROUPS + 1), dma(2 * GROUPS + 1),
        ],
        compiler_params=pltpu.CompilerParams(
            collective_id=0, has_side_effects=True, vmem_limit_bytes=63 * 2**20
        ),
        name="layers",
    )(
        ssm_input, gate_input, b_proj, c_proj, dt_raw.T, a_log.reshape(1, -1), skip.reshape(1, -1),
        norm_gain.reshape(1, -1), queries, keys, values, block_lists,
    )
    return pl.pallas_call(
        store_kernel,
        out_shape=outs,
        in_specs=[any_spec] * 2,
        out_specs=(any_spec, any_spec),
        scratch_shapes=[vmem((BLK, wide), BF16), vmem((BLK, heads), BF16), dma(4 * STORES)],
        compiler_params=pltpu.CompilerParams(vmem_limit_bytes=63 * 2**20),
        name="store",
    )(ssm, attn)


def solution(mesh):
    rows = P(("dp", "ctx"), None)
    in_specs = (rows, rows, rows, rows, rows, P(), P(), P(), rows, rows, rows, rows)
    return jax.shard_map(body, mesh=mesh, in_specs=in_specs, out_specs=(rows, rows), check_vma=False)
```

```python
import jax
import jax.numpy as jnp
from jax import lax
from jax.experimental import pallas as pl
from jax.experimental.pallas import tpu as pltpu
from jax.sharding import PartitionSpec as P

MESH = pl.DeviceIdType.MESH
F32 = jnp.float32
BF16 = jnp.bfloat16

SSM_HEADS = 64
HEAD_P = 64
GROUPS = 4
KVHEADS = 4
RATIO = 4
HEAD_D = 128
BLK = 128
NORM_EPS = 1e-05
MASKED = -1e30

CHIPS = 8
HALF = 512
COLS = 1024
PIECE = 128
PER_GROUP = 4
CHUNKS = GROUPS * PER_GROUP
UP_STEPS = 3
DOWN_STEPS = 5
LAG_NUM, LAG_DEN = 9, 2
KV_PARTS = 4
KV_ROWS = 2 * BLK // KV_PARTS
KV_TICKS = 2
ATTN_TICK = (26, 26, 31, 41, 41, 41, 44, 33)
ATTN_HEADS = 2
STORES = 2
ATTN_PIECES = KVHEADS * RATIO // ATTN_HEADS


def dot(a, b):
    return lax.dot_general(a, b, (((1,), (0,)), ((), ())), preferred_element_type=F32)


def dot_t(a, b):
    return lax.dot_general(a, b, (((1,), (1,)), ((), ())), preferred_element_type=F32)


def split(v):
    hi = v.astype(BF16)
    return hi, (v - hi.astype(F32)).astype(BF16)


def pick(y, table):
    value = table[0]
    for i in range(1, CHIPS):
        value = jnp.where(y == i, table[i], value)
    return value


def kernel(
    x_hbm, gate_hbm, b_hbm, c_hbm, dt_hbm, alog_hbm, skip_hbm, gain_hbm, q_hbm, k_hbm, v_hbm, list_hbm,
    ssm_v, attn_v,
    x, gate, b, cp, dtr, alog, skip, gain, q, lists,
    kv, stack, spread, bt, xs, a1, a2, local, sib, dec, dsib, chip, isend, pin, enter,
    in_sem,
    up_s, up_r, down_s, down_r, kvsib_s, kvsib_r, chain_s, chain_r, psib_s, psib_r, ex_s, ex_r,
):
    me = lax.axis_index("ctx")
    y = lax.div(me, 2)
    c = lax.rem(me, 2)
    oc = 1 - c
    above = lax.rem(y + 1, CHIPS) * 2 + c
    below = lax.rem(y + CHIPS - 1, CHIPS) * 2 + c
    other = y * 2 + oc

    barrier = pltpu.get_barrier_semaphore()
    for peer in (above, below, other):
        pl.semaphore_signal(barrier, inc=1, device_id={"ctx": peer}, device_id_type=MESH)

    loads = [
        pltpu.make_async_copy(src, dst, in_sem.at[i])
        for i, (src, dst) in enumerate(
            (
                (dt_hbm, dtr), (alog_hbm, alog), (skip_hbm, skip), (b_hbm, b),
                (k_hbm, kv.at[me, 0]), (v_hbm, kv.at[me, 1]), (x_hbm, x), (c_hbm, cp), (gate_hbm, gate),
                (gain_hbm, gain), (q_hbm, q), (list_hbm, lists),
            )
        )
    ]
    for load in loads:
        load.start()

    def remote(src, dst, send, recv, to):
        return pltpu.make_async_remote_copy(
            src_ref=src, dst_ref=dst, send_sem=send, recv_sem=recv, device_id={"ctx": to}, device_id_type=MESH
        )

    def kv_part(slot, part):
        rows = lax.rem(part, 2) * KV_ROWS
        return kv.at[slot, lax.div(part, 2), pl.ds(pl.multiple_of(rows, KV_ROWS), KV_ROWS)]

    def up_copy(e, ahead=0):
        slot = lax.rem(y - ahead - lax.div(e, KV_PARTS) + CHIPS, CHIPS) * 2 + c
        part = lax.rem(e, KV_PARTS)
        return remote(kv_part(slot, part), kv_part(slot, part), up_s.at[e], up_r.at[e], above), slot, part

    def down_copy(e, ahead=0):
        slot = lax.rem(y + ahead + lax.div(e, KV_PARTS), CHIPS) * 2 + c
        part = lax.rem(e, KV_PARTS)
        return remote(kv_part(slot, part), kv_part(slot, part), down_s.at[e], down_r.at[e], below), slot, part

    def up_sends(e):
        step = lax.div(e, KV_PARTS)
        return (y < CHIPS - 1) & (y >= step) & ((step < 2) | (y - step >= 3))

    def up_gets(e):
        step = lax.div(e, KV_PARTS)
        return (y >= 1 + step) & ((step < 2) | (y - 1 - step >= 3))

    def down_goes(source, step):
        return (source < 3) | ((source == 3) & (step < 4))

    def down_sends(e):
        step = lax.div(e, KV_PARTS)
        return down_goes(lax.rem(y + step, CHIPS), step)

    def down_gets(e):
        step = lax.div(e, KV_PARTS)
        return down_goes(lax.rem(y + 1 + step, CHIPS), step)

    def down_keeps(e):
        return (y + 1 + lax.div(e, KV_PARTS) >= CHIPS) & down_gets(e)

    def kv_sib(i, slot, part):
        return remote(kv_part(slot, part), kv_part(slot, part), kvsib_s.at[i], kvsib_r.at[i], other)

    UP0, DOWN0 = KV_PARTS, KV_PARTS + KV_PARTS * UP_STEPS

    r = lax.broadcasted_iota(jnp.int32, (SSM_HEADS, HALF), 0)
    h = lax.shift_right_logical(lax.broadcasted_iota(jnp.int32, (SSM_HEADS, HALF), 1), 6)
    for j in range(2 * GROUPS):
        spread[j] = (r - j * (HALF // HEAD_P) == h).astype(F32).astype(BF16)

    for load in loads[:4]:
        load.wait()
    raw = jnp.transpose(dtr[...])
    dt = jnp.maximum(raw, 0.0) + jnp.log1p(jnp.exp(-jnp.abs(raw)))
    rate = jnp.exp(alog[...])
    row = lax.broadcasted_iota(jnp.int32, (BLK, BLK), 0)
    col = lax.broadcasted_iota(jnp.int32, (BLK, BLK), 1)
    tri = row >= col
    cum = lax.dot_general(
        tri.astype(F32), -dt * rate, (((1,), (0,)), ((), ())), precision=lax.Precision.HIGHEST,
        preferred_element_type=F32,
    )
    up_to = jnp.exp(cum)
    l_hi, l_lo = split(jnp.broadcast_to(up_to[BLK - 1 : BLK], (16, SSM_HEADS)))
    s_hi, s_lo = split(jnp.broadcast_to(skip[...], (16, SSM_HEADS)))
    stack[0:BLK, :] = (dt * jnp.exp(-cum)).astype(BF16)
    stack[BLK : BLK + 16, :] = l_hi
    stack[BLK + 16 : BLK + 32, :] = l_lo
    stack[BLK + 32 : 2 * BLK + 32, :] = up_to.astype(BF16)
    stack[2 * BLK + 32 : 2 * BLK + 48, :] = s_hi
    stack[2 * BLK + 48 : 2 * BLK + 64, :] = s_lo
    for g in range(GROUPS):
        bt[g] = jnp.transpose(b[:, g * BLK : (g + 1) * BLK].astype(F32)).astype(BF16)
    for load in loads[4:7]:
        load.wait()

    pl.semaphore_wait(barrier, 3)
    for e in range(KV_PARTS):
        @pl.when(down_sends(e))
        def _(e=e):
            down_copy(e)[0].start()

        @pl.when(up_sends(e) & (y > 0))
        def _(e=e):
            up_copy(e)[0].start()

    def ex_d(g):
        some = pl.ds(g * PER_GROUP, PER_GROUP)
        return remote(dec.at[some], dsib.at[some], ex_s.at[g], ex_r.at[g], other)

    def ex_half(g, half):
        some = pl.ds(g * PER_GROUP, PER_GROUP)
        i = GROUPS + g
        return remote(local.at[half, some], sib.at[half, some], ex_s.at[i], ex_r.at[i], other)

    ex_rest = remote(local.at[0], sib.at[0], ex_s.at[2 * GROUPS], ex_r.at[2 * GROUPS], other)
    first = (c == 0).astype(F32)

    def own_state(g):
        for half in range(2):
            j = 2 * g + half
            cols = pl.ds(j * HALF, HALF)
            wide = dot(stack[0 : BLK + 32, :], spread[j])
            scaled = (x[:, cols].astype(F32) * wide[0:BLK]).astype(BF16)
            xs[:, cols] = scaled
            last = wide[BLK : BLK + 1] + wide[BLK + 16 : BLK + 17]
            state = dot(bt[g], scaled) * last
            for i in range(PER_GROUP):
                piece = slice(i * PIECE, (i + 1) * PIECE)
                local[half, g * PER_GROUP + i] = state[:, piece].astype(BF16)
                dec[g * PER_GROUP + i, half] = jnp.broadcast_to(last[:, piece], (8, PIECE))

    def chip_state(g):
        ex_d(g).wait_recv()
        ex_half(g, c).wait_recv()

        def one(i, carry):
            k = g * PER_GROUP + i
            mine, theirs = local[c, k].astype(F32), sib[c, k].astype(F32)
            d_mine, d_theirs = dec[k, c][0:1, :], dsib[k, c][0:1, :]
            value = first * (d_theirs * mine + theirs) + (1.0 - first) * (d_mine * theirs + mine)
            chip[k] = value

            @pl.when(y == 0)
            def _():
                isend[k] = value.astype(BF16)
                remote(isend.at[k], pin.at[c, k], chain_s.at[0], chain_r.at[k], above).start()
                pin[0, k] = jnp.zeros((BLK, PIECE), BF16)
                pin[1, k] = jnp.zeros((BLK, PIECE), BF16)

            return carry

        lax.fori_loop(0, PER_GROUP, one, 0)

    for g in range(GROUPS):
        own_state(g)
        ex_d(g).start()
        ex_half(g, oc).start()
        if g > 0:
            chip_state(g - 1)
    chip_state(GROUPS - 1)

    @pl.when(y == 0)
    def _():
        for e in range(KV_PARTS):
            up_copy(e)[0].start()

    @pl.when(c == 0)
    def _():
        ex_rest.start()

    for e in range(KV_PARTS):
        kv_sib(e, me, e).start()

    for load in loads[7:]:
        load.wait()

    def own_part(j):
        g = lax.div(j, 2)
        cols = pl.ds(pl.multiple_of(j * HALF, HALF), HALF)
        state_cols = pl.ds(pl.multiple_of(g * BLK, BLK), BLK)
        wide = dot(stack[BLK + 32 : 2 * BLK + 64, :], spread[j])
        uu = wide[0:BLK]
        sk = wide[BLK : BLK + 1] + wide[BLK + 16 : BLK + 17]
        products = dot_t(cp[:, state_cols], b[:, state_cols])
        mixing = jnp.where(tri, products, 0.0).astype(BF16)
        base = uu * dot(mixing, xs[:, cols]) + sk * x[:, cols].astype(F32)
        gt = gate[:, cols].astype(F32)
        act = gt / (1.0 + jnp.exp(-gt))
        a1[:, cols] = base * act
        a2[:, cols] = uu * act

    def attention(piece):
        blocks = [lists[0, i] for i in range(3)]
        slots = [me] + [jnp.where(i < 0, me, i) for i in blocks]
        biases = [jnp.where(i < 0, MASKED, 0.0).astype(F32) for i in blocks]
        kh = lax.div(piece * ATTN_HEADS, RATIO)
        cols = pl.ds(pl.multiple_of(kh * HEAD_D, HEAD_D), HEAD_D)
        heads = [
            pl.ds(pl.multiple_of((piece * ATTN_HEADS + i) * HEAD_D, HEAD_D), HEAD_D) for i in range(ATTN_HEADS)
        ]
        queries = jnp.concatenate([q[:, head] for head in heads], axis=0)
        scale = HEAD_D ** (-0.5)
        tris = jnp.concatenate([tri] * ATTN_HEADS, axis=0)
        scores = [dot_t(queries, kv[slot, 0, :, cols]) * scale for slot in slots]
        scores = [jnp.where(tris, scores[0], MASKED)] + [s + bias for s, bias in zip(scores[1:], biases)]
        top = jnp.maximum(jnp.maximum(scores[0], scores[1]), jnp.maximum(scores[2], scores[3]))
        top = jnp.max(top, axis=1, keepdims=True)
        weights = [jnp.exp(s - top) for s in scores]
        total = (weights[0] + weights[1]) + (weights[2] + weights[3])
        total = jnp.sum(total, axis=1, keepdims=True)
        acc = dot(weights[0].astype(BF16), kv[slots[0], 1, :, cols])
        for slot, weight in zip(slots[1:], weights[1:]):
            acc = acc + dot(weight.astype(BF16), kv[slot, 1, :, cols])
        out = (acc / total).astype(BF16)
        for i, head in enumerate(heads):
            attn_v[:, head] = out[i * BLK : (i + 1) * BLK]

    def psib(half, k):
        return remote(pin.at[half, k], pin.at[half, k], psib_s.at[0], psib_r.at[k], other)

    def finish(g):
        @pl.when((c == 1) & (g == 0))
        def _():
            ex_rest.wait_recv()

        cols = pl.ds(pl.multiple_of(g * COLS, COLS), COLS)
        state_cols = pl.ds(pl.multiple_of(g * BLK, BLK), BLK)

        @pl.when(y > 0)
        def _():
            for i in range(PER_GROUP):
                psib(oc, g * PER_GROUP + i).wait_recv()

        for half in range(2):
            for i in range(PER_GROUP):
                k = g * PER_GROUP + i
                place = slice((half * PER_GROUP + i) * PIECE, (half * PER_GROUP + i + 1) * PIECE)

                @pl.when(c == 0)
                def _(half=half, k=k, place=place):
                    enter[:, place] = pin[half, k]

                @pl.when(c == 1)
                def _(half=half, k=k, place=place):
                    came = dsib[k, half][0:1, :] * pin[half, k].astype(F32) + sib[half, k].astype(F32)
                    enter[:, place] = came.astype(BF16)

        gated = a1[:, cols] + a2[:, cols] * dot(cp[:, state_cols], enter[...])
        square = jnp.sum(gated * gated, axis=1, keepdims=True)
        scale = lax.rsqrt(square * (1.0 / COLS) + NORM_EPS)
        ssm_v[:, cols] = (gated * scale * gain[:, cols]).astype(BF16)

    reach = lax.div(y * LAG_NUM, LAG_DEN)
    attn_at = pick(y, ATTN_TICK)
    end = jnp.maximum(reach + CHUNKS + 1 + GROUPS, attn_at + ATTN_PIECES + 1)
    last_chip = y == CHIPS - 1
    late = y == 2
    late_from = (y >= 1) & (y <= 3)
    late_event = jnp.where(y == 1, 0, KV_PARTS)

    def tick(t, carry):
        k = t - reach

        @pl.when((y > 0) & (k >= 0) & (k < CHUNKS))
        def _():
            into = remote(isend.at[k], pin.at[c, k], chain_s.at[0], chain_r.at[k], above)
            into.wait_recv()

            @pl.when(y < CHIPS - 1)
            def _():
                d = dec[k, c][0:1, :] * dsib[k, c][0:1, :]
                isend[k] = (d * pin[c, k].astype(F32) + chip[k]).astype(BF16)
                into.start()

            psib(c, k).start()

        @pl.when(t < 2 * GROUPS)
        def _():
            own_part(t)

        @pl.when(late & (k == CHUNKS))
        def _():
            for e in range(KV_PARTS, 2 * KV_PARTS):
                up_copy(e)[0].start()

        in_chain = last_chip & (k > PER_GROUP) & (lax.rem(k, PER_GROUP) == 1) & (k <= CHUNKS + 1)
        behind_chain = jnp.logical_not(last_chip) & (k > CHUNKS) & (k <= CHUNKS + GROUPS)

        @pl.when(in_chain | behind_chain)
        def _():
            finish(jnp.where(last_chip, lax.div(k, PER_GROUP) - 1, k - CHUNKS - 1))

        e = lax.div(t, KV_TICKS) - 1
        now = (lax.rem(t, KV_TICKS) == 0) & (e >= 0)

        @pl.when(now & (e < KV_PARTS * DOWN_STEPS) & down_gets(jnp.maximum(e, 0)))
        def _():
            arrival, slot, part = down_copy(e, 1)
            arrival.wait_recv()

            @pl.when((e < KV_PARTS * (DOWN_STEPS - 1)) & down_sends(e + KV_PARTS))
            def _():
                down_copy(e + KV_PARTS)[0].start()

            @pl.when(down_keeps(e))
            def _():
                kv_sib(DOWN0 + e, slot, part).start()

        behind = late_from & (k > CHUNKS) & (k <= CHUNKS + KV_PARTS)
        u = jnp.where(behind, k - CHUNKS - 1 + late_event, e)
        due = behind | (now & (e < KV_PARTS * UP_STEPS) & (jnp.logical_not(late_from) | (e < late_event)))

        @pl.when(due & up_gets(jnp.maximum(u, 0)))
        def _():
            arrival, slot, part = up_copy(u, 1)
            arrival.wait_recv()

            @pl.when((u < KV_PARTS * (UP_STEPS - 1)) & up_sends(u + KV_PARTS) & jnp.logical_not(late))
            def _():
                up_copy(u + KV_PARTS)[0].start()

            kv_sib(UP0 + u, slot, part).start()

        @pl.when(t == attn_at)
        def _():
            for i in range(KV_PARTS):
                kv_sib(i, me, 0).wait_recv()

            def wait_up(i, carry):
                @pl.when(up_gets(i))
                def _():
                    kv_sib(UP0 + i, me, 0).wait_recv()
                return carry

            def wait_down(i, carry):
                @pl.when(down_keeps(i))
                def _():
                    kv_sib(DOWN0 + i, me, 0).wait_recv()
                return carry

            lax.fori_loop(0, KV_PARTS * UP_STEPS, wait_up, 0)
            lax.fori_loop(0, KV_PARTS * DOWN_STEPS, wait_down, 0)

        @pl.when((t >= attn_at) & (t < attn_at + ATTN_PIECES))
        def _():
            attention(t - attn_at)

        @pl.when(t == attn_at + ATTN_PIECES)
        def _():
            @pl.when(c == 0)
            def _():
                ex_rest.wait_send()

            for g in range(GROUPS):
                ex_d(g).wait_send()
                ex_half(g, oc).wait_send()

            def wait_up_sent(i, carry):
                @pl.when(up_sends(i))
                def _():
                    up_copy(i)[0].wait_send()

                @pl.when(up_gets(i))
                def _():
                    kv_sib(UP0 + i, me, 0).wait_send()
                return carry

            def wait_down_sent(i, carry):
                @pl.when(down_sends(i))
                def _():
                    down_copy(i)[0].wait_send()

                @pl.when(down_keeps(i))
                def _():
                    kv_sib(DOWN0 + i, me, 0).wait_send()
                return carry

            lax.fori_loop(0, KV_PARTS * UP_STEPS, wait_up_sent, 0)
            lax.fori_loop(0, KV_PARTS * DOWN_STEPS, wait_down_sent, 0)
            for i in range(KV_PARTS):
                kv_sib(i, me, i).wait_send()

        return carry

    lax.fori_loop(0, end, tick, 0)

    @pl.when(y > 0)
    def _():
        remote(pin.at[c], pin.at[c], psib_s.at[0], psib_r.at[0], other).wait_send()

    @pl.when(y < CHIPS - 1)
    def _():
        remote(isend, pin.at[c], chain_s.at[0], chain_r.at[0], above).wait_send()


def store_kernel(ssm, attn, ssm_out, attn_out, sem):
    copies = []
    for src, dst in ((ssm, ssm_out), (attn, attn_out)):
        for i in range(STORES):
            rows = pl.ds(i * (BLK // STORES), BLK // STORES)
            copies.append(pltpu.make_async_copy(src.at[rows], dst.at[rows], sem.at[len(copies)]))
    for copy in copies:
        copy.start()
    for copy in copies:
        copy.wait()


def body(ssm_input, gate_input, b_proj, c_proj, dt_raw, a_log, skip, norm_gain, queries, keys, values, block_lists):
    vmem = pltpu.VMEM
    dma = lambda n: pltpu.SemaphoreType.DMA((n,))
    wide = GROUPS * COLS
    heads = KVHEADS * RATIO * HEAD_D
    any_spec = pl.BlockSpec(memory_space=pl.ANY)
    vmem_spec = pl.BlockSpec(memory_space=pltpu.VMEM)
    outs = (jax.ShapeDtypeStruct((BLK, wide), BF16), jax.ShapeDtypeStruct((BLK, heads), BF16))
    ssm, attn = pl.pallas_call(
        kernel,
        out_shape=(vmem((BLK, wide), BF16), vmem((BLK, heads), BF16)),
        in_specs=[any_spec] * 12,
        out_specs=(vmem_spec, vmem_spec),
        scratch_shapes=[
            vmem((BLK, wide), BF16), vmem((BLK, wide), BF16), vmem((BLK, GROUPS * BLK), BF16),
            vmem((BLK, GROUPS * BLK), BF16), vmem((SSM_HEADS, BLK), F32), vmem((1, SSM_HEADS), F32),
            vmem((1, SSM_HEADS), F32), vmem((1, wide), F32), vmem((BLK, heads), BF16),
            pltpu.SMEM((1, 3), jnp.int32),
            vmem((2 * CHIPS, 2, BLK, KVHEADS * HEAD_D), BF16),
            vmem((2 * BLK + 64, SSM_HEADS), BF16), vmem((2 * GROUPS, SSM_HEADS, HALF), BF16),
            vmem((GROUPS, BLK, BLK), BF16),
            vmem((BLK, wide), BF16), vmem((BLK, wide), F32), vmem((BLK, wide), F32),
            vmem((2, CHUNKS, BLK, PIECE), BF16), vmem((2, CHUNKS, BLK, PIECE), BF16),
            vmem((CHUNKS, 2, 8, PIECE), F32), vmem((CHUNKS, 2, 8, PIECE), F32),
            vmem((CHUNKS, BLK, PIECE), F32), vmem((CHUNKS, BLK, PIECE), BF16),
            vmem((2, CHUNKS, BLK, PIECE), BF16), vmem((BLK, COLS), BF16),
            dma(12),
            dma(KV_PARTS * UP_STEPS), dma(KV_PARTS * UP_STEPS), dma(KV_PARTS * DOWN_STEPS),
            dma(KV_PARTS * DOWN_STEPS), dma(KV_PARTS * (1 + UP_STEPS + DOWN_STEPS)),
            dma(KV_PARTS * (1 + UP_STEPS + DOWN_STEPS)),
            dma(1), dma(CHUNKS), dma(1), dma(CHUNKS), dma(2 * GROUPS + 1), dma(2 * GROUPS + 1),
        ],
        compiler_params=pltpu.CompilerParams(
            collective_id=0, has_side_effects=True, vmem_limit_bytes=60 * 2**20
        ),
        name="layers",
    )(
        ssm_input, gate_input, b_proj, c_proj, dt_raw.T, a_log.reshape(1, -1), skip.reshape(1, -1),
        norm_gain.reshape(1, -1), queries, keys, values, block_lists,
    )
    return pl.pallas_call(
        store_kernel,
        out_shape=outs,
        in_specs=[vmem_spec] * 2,
        out_specs=(any_spec, any_spec),
        scratch_shapes=[dma(2 * STORES)],
        compiler_params=pltpu.CompilerParams(vmem_limit_bytes=4 * 2**20),
        name="store",
    )(ssm, attn)


def solution(mesh):
    rows = P(("dp", "ctx"), None)
    in_specs = (rows, rows, rows, rows, rows, P(), P(), P(), rows, rows, rows, rows)
    return jax.shard_map(body, mesh=mesh, in_specs=in_specs, out_specs=(rows, rows), check_vma=False)
```

```python
import jax
import jax.numpy as jnp
from jax import lax
from jax.experimental import pallas as pl
from jax.experimental.pallas import tpu as pltpu
from jax.sharding import PartitionSpec as P

MESH = pl.DeviceIdType.MESH
F32 = jnp.float32
BF16 = jnp.bfloat16

SSM_HEADS = 64
HEAD_P = 64
GROUPS = 4
KVHEADS = 4
RATIO = 4
HEAD_D = 128
BLK = 128
NORM_EPS = 1e-05
MASKED = -1e30
LOG2_E = 1.4426950408889634

CHIPS = 8
HALF = 512
COLS = 1024
PIECE = 128
PER_GROUP = 4
CHUNKS = GROUPS * PER_GROUP
CUTS = 2
CUT = BLK // CUTS
UP_STEPS = 3
DOWN_STEPS = 5
LAG_NUM, LAG_DEN = 9, 2
KV_PARTS = 4
KV_ROWS = 2 * BLK // KV_PARTS
KV_TICKS = 2
ATTN_TICK = (26, 26, 31, 41, 41, 41, 44, 33)
DRAIN_TICK = (28, 28, 33, 43, 43, 43, 42, 41)
ATTN_KEY_HEADS = 2
STORES = 2
ATTN_PIECES = KVHEADS // ATTN_KEY_HEADS


def dot(a, b):
    return lax.dot_general(a, b, (((1,), (0,)), ((), ())), preferred_element_type=F32)


def dot_t(a, b):
    return lax.dot_general(a, b, (((1,), (1,)), ((), ())), preferred_element_type=F32)


def split(v):
    hi = v.astype(BF16)
    return hi, (v - hi.astype(F32)).astype(BF16)


def pick(y, table):
    value = table[0]
    for i in range(1, CHIPS):
        value = jnp.where(y == i, table[i], value)
    return value


def kernel(
    x_hbm, gate_hbm, b_hbm, c_hbm, dt_hbm, alog_hbm, skip_hbm, gain_hbm, q_hbm, k_hbm, v_hbm, list_hbm,
    ssm_v, attn_v,
    x, gate, b, cp, dtr, alog, skip, gain, q, lists,
    kv, stack, spread, bt, xs, a1, a2, local, sib, dec, dsib, chip, isend, pin,
    in_sem,
    up_s, up_r, down_s, down_r, kvsib_s, kvsib_r, chain_s, chain_r, psib_s, psib_r, ex_s, ex_r,
):
    me = lax.axis_index("ctx")
    y = lax.div(me, 2)
    c = lax.rem(me, 2)
    oc = 1 - c
    above = lax.rem(y + 1, CHIPS) * 2 + c
    below = lax.rem(y + CHIPS - 1, CHIPS) * 2 + c
    other = y * 2 + oc

    barrier = pltpu.get_barrier_semaphore()
    for peer in (above, below, other):
        pl.semaphore_signal(barrier, inc=1, device_id={"ctx": peer}, device_id_type=MESH)

    loads = [
        pltpu.make_async_copy(src, dst, in_sem.at[i])
        for i, (src, dst) in enumerate(
            (
                (dt_hbm, dtr), (alog_hbm, alog), (skip_hbm, skip), (b_hbm, b),
                (k_hbm, kv.at[me, 0]), (v_hbm, kv.at[me, 1]), (x_hbm, x), (c_hbm, cp), (gate_hbm, gate),
                (gain_hbm, gain), (q_hbm, q), (list_hbm, lists),
            )
        )
    ]
    for load in loads:
        load.start()

    def remote(src, dst, send, recv, to):
        return pltpu.make_async_remote_copy(
            src_ref=src, dst_ref=dst, send_sem=send, recv_sem=recv, device_id={"ctx": to}, device_id_type=MESH
        )

    def kv_part(slot, part):
        rows = lax.rem(part, 2) * KV_ROWS
        return kv.at[slot, lax.div(part, 2), pl.ds(pl.multiple_of(rows, KV_ROWS), KV_ROWS)]

    def up_copy(e, ahead=0):
        slot = lax.rem(y - ahead - lax.div(e, KV_PARTS) + CHIPS, CHIPS) * 2 + c
        part = lax.rem(e, KV_PARTS)
        return remote(kv_part(slot, part), kv_part(slot, part), up_s.at[e], up_r.at[e], above), slot, part

    def down_copy(e, ahead=0):
        slot = lax.rem(y + ahead + lax.div(e, KV_PARTS), CHIPS) * 2 + c
        part = lax.rem(e, KV_PARTS)
        return remote(kv_part(slot, part), kv_part(slot, part), down_s.at[e], down_r.at[e], below), slot, part

    def up_sends(e):
        step = lax.div(e, KV_PARTS)
        return (y < CHIPS - 1) & (y >= step) & ((step < 2) | (y - step >= 4))

    def up_gets(e):
        step = lax.div(e, KV_PARTS)
        return (y >= 1 + step) & ((step < 2) | (y - 1 - step >= 4))

    def down_sends(e):
        step = lax.div(e, KV_PARTS)
        return lax.rem(y + step, CHIPS) < CHIPS // 2

    def down_gets(e):
        step = lax.div(e, KV_PARTS)
        return lax.rem(y + 1 + step, CHIPS) < CHIPS // 2

    def down_keeps(e):
        return (y + 1 + lax.div(e, KV_PARTS) >= CHIPS) & down_gets(e)

    def kv_sib(i, slot, part):
        return remote(kv_part(slot, part), kv_part(slot, part), kvsib_s.at[i], kvsib_r.at[i], other)

    UP0, DOWN0 = KV_PARTS, KV_PARTS + KV_PARTS * UP_STEPS

    r = lax.broadcasted_iota(jnp.int32, (SSM_HEADS, HALF), 0)
    h = lax.shift_right_logical(lax.broadcasted_iota(jnp.int32, (SSM_HEADS, HALF), 1), 6)
    for j in range(2 * GROUPS):
        spread[j] = (r - j * (HALF // HEAD_P) == h).astype(F32).astype(BF16)

    for load in loads[:4]:
        load.wait()
    raw = jnp.transpose(dtr[...])
    dt = jnp.maximum(raw, 0.0) + jnp.log1p(jnp.exp(-jnp.abs(raw)))
    rate = jnp.exp(alog[...])
    row = lax.broadcasted_iota(jnp.int32, (BLK, BLK), 0)
    col = lax.broadcasted_iota(jnp.int32, (BLK, BLK), 1)
    tri = row >= col
    cum = lax.dot_general(
        tri.astype(F32), -dt * rate, (((1,), (0,)), ((), ())), precision=lax.Precision.HIGHEST,
        preferred_element_type=F32,
    )
    up_to = jnp.exp(cum)
    l_hi, l_lo = split(jnp.broadcast_to(up_to[BLK - 1 : BLK], (16, SSM_HEADS)))
    s_hi, s_lo = split(jnp.broadcast_to(skip[...], (16, SSM_HEADS)))
    stack[0:BLK, :] = (dt * jnp.exp(-cum)).astype(BF16)
    stack[BLK : BLK + 16, :] = l_hi
    stack[BLK + 16 : BLK + 32, :] = l_lo
    stack[BLK + 32 : 2 * BLK + 32, :] = up_to.astype(BF16)
    stack[2 * BLK + 32 : 2 * BLK + 48, :] = s_hi
    stack[2 * BLK + 48 : 2 * BLK + 64, :] = s_lo
    for g in range(GROUPS):
        bt[g] = jnp.transpose(b[:, g * BLK : (g + 1) * BLK].astype(F32)).astype(BF16)
    for load in loads[4:7]:
        load.wait()

    def ex_d(g):
        some = pl.ds(g * PER_GROUP, PER_GROUP)
        return remote(dec.at[some], dsib.at[some], ex_s.at[g], ex_r.at[g], other)

    def ex_half(g, half):
        some = pl.ds(g * PER_GROUP, PER_GROUP)
        i = GROUPS + g
        return remote(local.at[half, some], sib.at[half, some], ex_s.at[i], ex_r.at[i], other)

    ex_rest = remote(local.at[0], sib.at[0], ex_s.at[2 * GROUPS], ex_r.at[2 * GROUPS], other)
    first = (c == 0).astype(F32)

    def link(k, i):
        rows = pl.ds(i * CUT, CUT)
        n = k * CUTS + i
        return remote(isend.at[k, rows], pin.at[c, k, rows], chain_s.at[0], chain_r.at[n], above)

    def own_state(g):
        for half in range(2):
            j = 2 * g + half
            cols = pl.ds(j * HALF, HALF)
            wide = dot(stack[0 : BLK + 32, :], spread[j])
            scaled = (x[:, cols].astype(F32) * wide[0:BLK]).astype(BF16)
            xs[:, cols] = scaled
            last = wide[BLK : BLK + 1] + wide[BLK + 16 : BLK + 17]
            state = dot(bt[g], scaled) * last
            for i in range(PER_GROUP):
                piece = slice(i * PIECE, (i + 1) * PIECE)
                local[half, g * PER_GROUP + i] = state[:, piece].astype(BF16)
                dec[g * PER_GROUP + i, half] = jnp.broadcast_to(last[:, piece], (8, PIECE))

    def chip_state(g):
        ex_d(g).wait_recv()
        ex_half(g, c).wait_recv()

        def one(i, carry):
            k = g * PER_GROUP + i
            mine, theirs = local[c, k].astype(F32), sib[c, k].astype(F32)
            d_mine, d_theirs = dec[k, c][0:1, :], dsib[k, c][0:1, :]
            value = first * (d_theirs * mine + theirs) + (1.0 - first) * (d_mine * theirs + mine)
            chip[k] = value

            @pl.when(y == 0)
            def _():
                isend[k] = value.astype(BF16)
                for cut in range(CUTS):
                    link(k, cut).start()
                pin[0, k] = jnp.zeros((BLK, PIECE), BF16)
                pin[1, k] = jnp.zeros((BLK, PIECE), BF16)

            return carry

        lax.fori_loop(0, PER_GROUP, one, 0)

    own_state(0)
    pl.semaphore_wait(barrier, 3)
    ex_d(0).start()
    ex_half(0, oc).start()
    for e in range(KV_PARTS):
        @pl.when(down_sends(e))
        def _(e=e):
            down_copy(e)[0].start()

        @pl.when(up_sends(e) & (y > 0))
        def _(e=e):
            up_copy(e)[0].start()

    for g in range(1, GROUPS):
        own_state(g)
        ex_d(g).start()
        ex_half(g, oc).start()
        chip_state(g - 1)
    chip_state(GROUPS - 1)

    @pl.when(y == 0)
    def _():
        for e in range(KV_PARTS):
            up_copy(e)[0].start()

    @pl.when(c == 0)
    def _():
        ex_rest.start()

    for e in range(KV_PARTS):
        kv_sib(e, me, e).start()

    for load in loads[7:]:
        load.wait()

    def own_part(j):
        g = lax.div(j, 2)
        cols = pl.ds(pl.multiple_of(j * HALF, HALF), HALF)
        state_cols = pl.ds(pl.multiple_of(g * BLK, BLK), BLK)
        wide = dot(stack[BLK + 32 : 2 * BLK + 64, :], spread[j])
        uu = wide[0:BLK]
        sk = wide[BLK : BLK + 1] + wide[BLK + 16 : BLK + 17]
        products = dot_t(cp[:, state_cols], b[:, state_cols])
        mixing = jnp.where(tri, products, 0.0).astype(BF16)
        base = uu * dot(mixing, xs[:, cols]) + sk * x[:, cols].astype(F32)
        gt = gate[:, cols].astype(F32)
        act = gt / (1.0 + jnp.exp(-gt))
        a1[:, cols] = base * act
        a2[:, cols] = uu * act

    def attention(piece):
        blocks = [lists[0, i] for i in range(3)]
        slots = [me] + [jnp.where(i < 0, me, i) for i in blocks]
        biases = [jnp.where(i < 0, MASKED, 0.0).astype(F32) for i in blocks]
        tris = jnp.concatenate([tri] * RATIO, axis=0)
        scale = HEAD_D ** (-0.5) * LOG2_E
        for h in range(ATTN_KEY_HEADS):
            kh = piece * ATTN_KEY_HEADS + h
            cols = pl.ds(pl.multiple_of(kh * HEAD_D, HEAD_D), HEAD_D)
            heads = [pl.ds(pl.multiple_of((kh * RATIO + i) * HEAD_D, HEAD_D), HEAD_D) for i in range(RATIO)]
            queries = jnp.concatenate([q[:, head] for head in heads], axis=0)
            keys = jnp.concatenate([kv[slot, 0, :, cols] for slot in slots], axis=0)
            values = jnp.concatenate([kv[slot, 1, :, cols] for slot in slots], axis=0)
            values = jnp.concatenate([values, jnp.ones(values.shape, BF16)], axis=1)
            scores = dot_t(queries, keys)
            scores = [scores[:, i * BLK : (i + 1) * BLK] for i in range(4)]
            scores = [jnp.where(tris, scores[0], MASKED)] + [s + bias for s, bias in zip(scores[1:], biases)]
            top = jnp.maximum(jnp.maximum(scores[0], scores[1]), jnp.maximum(scores[2], scores[3]))
            top = jnp.max(top, axis=1, keepdims=True)
            weights = jnp.concatenate([jnp.exp2((s - top) * scale).astype(BF16) for s in scores], axis=1)
            acc = dot(weights, values)
            out = (acc[:, :HEAD_D] / acc[:, HEAD_D:]).astype(BF16)
            for i, head in enumerate(heads):
                attn_v[:, head] = out[i * BLK : (i + 1) * BLK]

    def psib(half, k):
        return remote(pin.at[half, k], pin.at[half, k], psib_s.at[0], psib_r.at[k], other)

    def finish(g):
        cols = pl.ds(pl.multiple_of(g * COLS, COLS), COLS)
        state_cols = pl.ds(pl.multiple_of(g * BLK, BLK), BLK)

        @pl.when(y > 0)
        def _():
            for i in range(PER_GROUP):
                psib(oc, g * PER_GROUP + i).wait_recv()

        def part(state):
            gated = a1[:, cols] + a2[:, cols] * dot(cp[:, state_cols], state)
            square = jnp.sum(gated * gated, axis=1, keepdims=True)
            scale = lax.rsqrt(square * (1.0 / COLS) + NORM_EPS)
            ssm_v[:, cols] = (gated * scale * gain[:, cols]).astype(BF16)

        def entering(half, i):
            k = g * PER_GROUP + i
            came = pin[half, k].astype(F32)
            return (dsib[k, half][0:1, :] * came + sib[half, k].astype(F32)).astype(BF16)

        pieces = [(half, i) for half in range(2) for i in range(PER_GROUP)]

        @pl.when(c == 0)
        def _():
            part(jnp.concatenate([pin[half, g * PER_GROUP + i] for half, i in pieces], axis=1))

        @pl.when(c == 1)
        def _():
            part(jnp.concatenate([entering(half, i) for half, i in pieces], axis=1))


    reach = lax.div(y * LAG_NUM, LAG_DEN)
    attn_at = pick(y, ATTN_TICK)
    last_chip = y == CHIPS - 1
    drain_at = pick(y, DRAIN_TICK)
    behind = jnp.where(last_chip, CHUNKS + 2, CHUNKS + 1 + GROUPS)
    end = jnp.maximum(jnp.maximum(reach + behind, attn_at + ATTN_PIECES), drain_at + 1)
    late = y == 2
    late_from = (y >= 1) & (y <= 3)
    late_event = jnp.where(y == 1, 0, KV_PARTS)

    def tick(t, carry):
        k = t - reach

        @pl.when((y > 0) & (k >= 0) & (k < CHUNKS))
        def _():
            for cut in range(CUTS):
                link(k, cut).wait_recv()

                @pl.when(y < CHIPS - 1)
                def _(cut=cut):
                    rows = slice(cut * CUT, (cut + 1) * CUT)
                    d = dec[k, c][0:1, :] * dsib[k, c][0:1, :]
                    isend[k, rows] = (d * pin[c, k, rows].astype(F32) + chip[k, rows]).astype(BF16)
                    link(k, cut).start()

            psib(c, k).start()

        @pl.when(t < 2 * GROUPS)
        def _():
            own_part(t)

        @pl.when(late & (k == CHUNKS))
        def _():
            for e in range(KV_PARTS, 2 * KV_PARTS):
                up_copy(e)[0].start()

        in_chain = last_chip & (k > PER_GROUP) & (lax.rem(k, PER_GROUP) == 1) & (k <= CHUNKS + 1)

        @pl.when((c == 1) & (k == jnp.where(last_chip, PER_GROUP + 1, CHUNKS + 1)))
        def _():
            ex_rest.wait_recv()

        @pl.when(in_chain)
        def _():
            finish(lax.div(k, PER_GROUP) - 1)

        @pl.when(jnp.logical_not(last_chip) & (k == CHUNKS + 1))
        def _():
            for g in range(GROUPS):
                finish(g)

        e = lax.div(t, KV_TICKS) - 1
        now = (lax.rem(t, KV_TICKS) == 0) & (e >= 0)

        @pl.when(now & (e < KV_PARTS * DOWN_STEPS) & down_gets(jnp.maximum(e, 0)))
        def _():
            arrival, slot, part = down_copy(e, 1)
            arrival.wait_recv()

            @pl.when((e < KV_PARTS * (DOWN_STEPS - 1)) & down_sends(e + KV_PARTS))
            def _():
                down_copy(e + KV_PARTS)[0].start()

            @pl.when(down_keeps(e))
            def _():
                kv_sib(DOWN0 + e, slot, part).start()

        behind = late_from & (k > CHUNKS) & (k <= CHUNKS + KV_PARTS)
        u = jnp.where(behind, k - CHUNKS - 1 + late_event, e)
        due = behind | (now & (e < KV_PARTS * UP_STEPS) & (jnp.logical_not(late_from) | (e < late_event)))

        @pl.when(due & up_gets(jnp.maximum(u, 0)))
        def _():
            arrival, slot, part = up_copy(u, 1)
            arrival.wait_recv()

            @pl.when((u < KV_PARTS * (UP_STEPS - 1)) & up_sends(u + KV_PARTS) & jnp.logical_not(late))
            def _():
                up_copy(u + KV_PARTS)[0].start()

            kv_sib(UP0 + u, slot, part).start()

        @pl.when(t == attn_at)
        def _():
            for i in range(KV_PARTS):
                kv_sib(i, me, 0).wait_recv()

            def wait_up(i, carry):
                @pl.when(up_gets(i))
                def _():
                    kv_sib(UP0 + i, me, 0).wait_recv()
                return carry

            def wait_down(i, carry):
                @pl.when(down_keeps(i))
                def _():
                    kv_sib(DOWN0 + i, me, 0).wait_recv()
                return carry

            lax.fori_loop(0, KV_PARTS * UP_STEPS, wait_up, 0)
            lax.fori_loop(0, KV_PARTS * DOWN_STEPS, wait_down, 0)

        @pl.when((t >= attn_at) & (t < attn_at + ATTN_PIECES))
        def _():
            attention(t - attn_at)

        @pl.when(t == drain_at)
        def _():
            @pl.when(c == 0)
            def _():
                ex_rest.wait_send()

            for g in range(GROUPS):
                ex_d(g).wait_send()
                ex_half(g, oc).wait_send()

            def wait_up_sent(i, carry):
                @pl.when(up_sends(i))
                def _():
                    up_copy(i)[0].wait_send()

                @pl.when(up_gets(i))
                def _():
                    kv_sib(UP0 + i, me, 0).wait_send()
                return carry

            def wait_down_sent(i, carry):
                @pl.when(down_sends(i))
                def _():
                    down_copy(i)[0].wait_send()

                @pl.when(down_keeps(i))
                def _():
                    kv_sib(DOWN0 + i, me, 0).wait_send()
                return carry

            lax.fori_loop(0, KV_PARTS * UP_STEPS, wait_up_sent, 0)
            lax.fori_loop(0, KV_PARTS * DOWN_STEPS, wait_down_sent, 0)
            for i in range(KV_PARTS):
                kv_sib(i, me, i).wait_send()

        return carry

    lax.fori_loop(0, end, tick, 0)

    @pl.when(y > 0)
    def _():
        remote(pin.at[c], pin.at[c], psib_s.at[0], psib_r.at[0], other).wait_send()

    @pl.when(y < CHIPS - 1)
    def _():
        remote(isend, pin.at[c], chain_s.at[0], chain_r.at[0], above).wait_send()


def store_kernel(ssm, attn, ssm_out, attn_out, sem):
    copies = []
    for src, dst in ((ssm, ssm_out), (attn, attn_out)):
        for i in range(STORES):
            rows = pl.ds(i * (BLK // STORES), BLK // STORES)
            copies.append(pltpu.make_async_copy(src.at[rows], dst.at[rows], sem.at[len(copies)]))
    for copy in copies:
        copy.start()
    for copy in copies:
        copy.wait()


def body(ssm_input, gate_input, b_proj, c_proj, dt_raw, a_log, skip, norm_gain, queries, keys, values, block_lists):
    vmem = pltpu.VMEM
    dma = lambda n: pltpu.SemaphoreType.DMA((n,))
    wide = GROUPS * COLS
    heads = KVHEADS * RATIO * HEAD_D
    any_spec = pl.BlockSpec(memory_space=pl.ANY)
    vmem_spec = pl.BlockSpec(memory_space=pltpu.VMEM)
    outs = (jax.ShapeDtypeStruct((BLK, wide), BF16), jax.ShapeDtypeStruct((BLK, heads), BF16))
    ssm, attn = pl.pallas_call(
        kernel,
        out_shape=(vmem((BLK, wide), BF16), vmem((BLK, heads), BF16)),
        in_specs=[any_spec] * 12,
        out_specs=(vmem_spec, vmem_spec),
        scratch_shapes=[
            vmem((BLK, wide), BF16), vmem((BLK, wide), BF16), vmem((BLK, GROUPS * BLK), BF16),
            vmem((BLK, GROUPS * BLK), BF16), vmem((SSM_HEADS, BLK), F32), vmem((1, SSM_HEADS), F32),
            vmem((1, SSM_HEADS), F32), vmem((1, wide), F32), vmem((BLK, heads), BF16),
            pltpu.SMEM((1, 3), jnp.int32),
            vmem((2 * CHIPS, 2, BLK, KVHEADS * HEAD_D), BF16),
            vmem((2 * BLK + 64, SSM_HEADS), BF16), vmem((2 * GROUPS, SSM_HEADS, HALF), BF16),
            vmem((GROUPS, BLK, BLK), BF16),
            vmem((BLK, wide), BF16), vmem((BLK, wide), F32), vmem((BLK, wide), F32),
            vmem((2, CHUNKS, BLK, PIECE), BF16), vmem((2, CHUNKS, BLK, PIECE), BF16),
            vmem((CHUNKS, 2, 8, PIECE), F32), vmem((CHUNKS, 2, 8, PIECE), F32),
            vmem((CHUNKS, BLK, PIECE), F32), vmem((CHUNKS, BLK, PIECE), BF16),
            vmem((2, CHUNKS, BLK, PIECE), BF16),
            dma(12),
            dma(KV_PARTS * UP_STEPS), dma(KV_PARTS * UP_STEPS), dma(KV_PARTS * DOWN_STEPS),
            dma(KV_PARTS * DOWN_STEPS), dma(KV_PARTS * (1 + UP_STEPS + DOWN_STEPS)),
            dma(KV_PARTS * (1 + UP_STEPS + DOWN_STEPS)),
            dma(1), dma(CHUNKS * CUTS), dma(1), dma(CHUNKS), dma(2 * GROUPS + 1), dma(2 * GROUPS + 1),
        ],
        compiler_params=pltpu.CompilerParams(
            collective_id=0, has_side_effects=True, vmem_limit_bytes=60 * 2**20
        ),
        name="layers",
    )(
        ssm_input, gate_input, b_proj, c_proj, dt_raw.T, a_log.reshape(1, -1), skip.reshape(1, -1),
        norm_gain.reshape(1, -1), queries, keys, values, block_lists,
    )
    return pl.pallas_call(
        store_kernel,
        out_shape=outs,
        in_specs=[vmem_spec] * 2,
        out_specs=(any_spec, any_spec),
        scratch_shapes=[dma(2 * STORES)],
        compiler_params=pltpu.CompilerParams(vmem_limit_bytes=4 * 2**20),
        name="store",
    )(ssm, attn)


def solution(mesh):
    rows = P(("dp", "ctx"), None)
    in_specs = (rows, rows, rows, rows, rows, P(), P(), P(), rows, rows, rows, rows)
    return jax.shard_map(body, mesh=mesh, in_specs=in_specs, out_specs=(rows, rows), check_vma=False)
```

```python
import jax
import jax.numpy as jnp
from jax import lax
from jax.experimental import pallas as pl
from jax.experimental.pallas import tpu as pltpu
from jax.sharding import PartitionSpec as P

MESH = pl.DeviceIdType.MESH
F32 = jnp.float32
BF16 = jnp.bfloat16

SSM_HEADS = 64
HEAD_P = 64
GROUPS = 4
KVHEADS = 4
RATIO = 4
HEAD_D = 128
BLK = 128
NORM_EPS = 1e-05
MASKED = -1e30
LOG2_E = 1.4426950408889634

CHIPS = 8
HALF = 512
COLS = 1024
PIECE = 128
PER_GROUP = 4
CHUNKS = GROUPS * PER_GROUP
UP_STEPS = 3
DOWN_STEPS = 5
LAG_NUM, LAG_DEN = 10, 3
KV_PARTS = 4
KV_TICKS = 2
KV_FIRST = 4
LATE = 4
FIRST_TICK = 22
NORM_TICK = (23, 23, 22, 26, 33, 38, 37, 35)
ATTN_TICK = (32, 28, 31, 43, 43, 43, 43, 39)
ATTN_KEY_HEADS = 4
STORES = 2
ATTN_PIECES = KVHEADS // ATTN_KEY_HEADS


def dot(a, b):
    return lax.dot_general(a, b, (((1,), (0,)), ((), ())), preferred_element_type=F32)


def dot_t(a, b):
    return lax.dot_general(a, b, (((1,), (1,)), ((), ())), preferred_element_type=F32)


def split(v):
    hi = v.astype(BF16)
    return hi, (v - hi.astype(F32)).astype(BF16)


def pick(y, table):
    value = table[0]
    for i in range(1, CHIPS):
        value = jnp.where(y == i, table[i], value)
    return value


def kernel(
    x_hbm, gate_hbm, b_hbm, c_hbm, dt_hbm, alog_hbm, skip_hbm, gain_hbm, q_hbm, k_hbm, v_hbm, list_hbm,
    ssm_v, attn_v,
    x, gate, b, cp, dtr, alog, skip, gain, q, lists,
    kv, stack, spread, bt, xs, a1, a2, local, sib, dec, dsib, chip, isend, pin,
    in_sem,
    up_s, up_r, down_s, down_r, kvsib_s, kvsib_r, chain_s, chain_r, psib_s, psib_r, ex_s, ex_r,
):
    me = lax.axis_index("ctx")
    y = lax.div(me, 2)
    c = lax.rem(me, 2)
    oc = 1 - c
    above = lax.rem(y + 1, CHIPS) * 2 + c
    below = lax.rem(y + CHIPS - 1, CHIPS) * 2 + c
    other = y * 2 + oc

    barrier = pltpu.get_barrier_semaphore()
    for peer in (above, below, other):
        pl.semaphore_signal(barrier, inc=1, device_id={"ctx": peer}, device_id_type=MESH)

    loads = [
        pltpu.make_async_copy(src, dst, in_sem.at[i])
        for i, (src, dst) in enumerate(
            (
                (dt_hbm, dtr), (alog_hbm, alog), (skip_hbm, skip), (b_hbm, b),
                (k_hbm, kv.at[me, 0]), (v_hbm, kv.at[me, 1]), (x_hbm, x), (c_hbm, cp), (gate_hbm, gate),
                (gain_hbm, gain), (q_hbm, q), (list_hbm, lists),
            )
        )
    ]
    for load in loads:
        load.start()

    def remote(src, dst, send, recv, to):
        return pltpu.make_async_remote_copy(
            src_ref=src, dst_ref=dst, send_sem=send, recv_sem=recv, device_id={"ctx": to}, device_id_type=MESH
        )

    def kv_piece(chip_y, part):
        return kv.at[chip_y * 2 + lax.rem(part, 2), lax.div(part, 2)]

    def up_copy(e, ahead=0):
        from_y = lax.rem(y - ahead - lax.div(e, KV_PARTS) + CHIPS, CHIPS)
        piece = kv_piece(from_y, lax.rem(e, KV_PARTS))
        return remote(piece, piece, up_s.at[e], up_r.at[e], above), piece

    def down_copy(e, ahead=0):
        from_y = lax.rem(y + ahead + lax.div(e, KV_PARTS), CHIPS)
        piece = kv_piece(from_y, lax.rem(e, KV_PARTS))
        return remote(piece, piece, down_s.at[e], down_r.at[e], below), piece

    def up_goes(source, e):
        values = lax.rem(e, KV_PARTS) >= KV_PARTS // 2
        return (e < 2 * KV_PARTS) | ((source >= 4) & values)

    def down_goes(source, e):
        keys = lax.rem(e, KV_PARTS) < KV_PARTS // 2
        return (source < 4) | ((source == 4) & keys)

    def up_sends(e):
        step = lax.div(e, KV_PARTS)
        return (y < CHIPS - 1) & (y >= step) & up_goes(y - step, e)

    def up_gets(e):
        step = lax.div(e, KV_PARTS)
        return (y >= 1 + step) & up_goes(y - 1 - step, e)

    def down_sends(e):
        step = lax.div(e, KV_PARTS)
        return down_goes(lax.rem(y + step, CHIPS), e)

    def down_gets(e):
        step = lax.div(e, KV_PARTS)
        return down_goes(lax.rem(y + 1 + step, CHIPS), e)

    def down_keeps(e):
        return (y + 1 + lax.div(e, KV_PARTS) >= CHIPS) & down_gets(e)

    def kv_sib(i, piece):
        return remote(piece, piece, kvsib_s.at[i], kvsib_r.at[i], other)

    def own_sib(i):
        return kv_sib(i, kv.at[me, i])

    UP0, DOWN0 = 2, 2 + KV_PARTS * UP_STEPS

    r = lax.broadcasted_iota(jnp.int32, (SSM_HEADS, HALF), 0)
    h = lax.shift_right_logical(lax.broadcasted_iota(jnp.int32, (SSM_HEADS, HALF), 1), 6)
    for j in range(2 * GROUPS):
        spread[j] = (r - j * (HALF // HEAD_P) == h).astype(F32).astype(BF16)

    for load in loads[:4]:
        load.wait()
    raw = jnp.transpose(dtr[...])
    dt = jnp.maximum(raw, 0.0) + jnp.log1p(jnp.exp(-jnp.abs(raw)))
    rate = jnp.exp(alog[...])
    row = lax.broadcasted_iota(jnp.int32, (BLK, BLK), 0)
    col = lax.broadcasted_iota(jnp.int32, (BLK, BLK), 1)
    tri = row >= col
    cum = lax.dot_general(
        tri.astype(F32), -dt * rate, (((1,), (0,)), ((), ())), precision=lax.Precision.HIGHEST,
        preferred_element_type=F32,
    )
    up_to = jnp.exp(cum)
    l_hi, l_lo = split(jnp.broadcast_to(up_to[BLK - 1 : BLK], (16, SSM_HEADS)))
    s_hi, s_lo = split(jnp.broadcast_to(skip[...], (16, SSM_HEADS)))
    stack[0:BLK, :] = (dt * jnp.exp(-cum)).astype(BF16)
    stack[BLK : BLK + 16, :] = l_hi
    stack[BLK + 16 : BLK + 32, :] = l_lo
    stack[BLK + 32 : 2 * BLK + 32, :] = up_to.astype(BF16)
    stack[2 * BLK + 32 : 2 * BLK + 48, :] = s_hi
    stack[2 * BLK + 48 : 2 * BLK + 64, :] = s_lo
    for g in range(GROUPS):
        bt[g] = jnp.transpose(b[:, g * BLK : (g + 1) * BLK].astype(F32)).astype(BF16)
    for load in loads[4:7]:
        load.wait()

    def ex_d(g):
        some = pl.ds(g * PER_GROUP, PER_GROUP)
        return remote(dec.at[some], dsib.at[some], ex_s.at[g], ex_r.at[g], other)

    def ex_state(g):
        some = pl.ds(g * PER_GROUP, PER_GROUP)
        i = GROUPS + g
        return remote(local.at[some], sib.at[some], ex_s.at[i], ex_r.at[i], other)

    def link(k, half):
        n = k * 2 + half
        return remote(isend.at[k, half], pin.at[k, half], chain_s.at[0], chain_r.at[n], above)

    def own_state(g):
        for half in range(2):
            j = 2 * g + half
            cols = pl.ds(j * HALF, HALF)
            wide = dot(stack[0 : BLK + 32, :], spread[j])
            scaled = (x[:, cols].astype(F32) * wide[0:BLK]).astype(BF16)
            xs[:, cols] = scaled
            last = wide[BLK : BLK + 1] + wide[BLK + 16 : BLK + 17]
            state = dot(bt[g], scaled) * last
            for i in range(PER_GROUP):
                piece = slice(i * PIECE, (i + 1) * PIECE)
                local[g * PER_GROUP + i, half] = state[:, piece].astype(BF16)
                dec[g * PER_GROUP + i, half] = jnp.broadcast_to(last[:, piece], (8, PIECE))

    def chip_state(g):
        ex_d(g).wait_recv()
        ex_state(g).wait_recv()

        def one(i, carry):
            k = g * PER_GROUP + i
            for half in range(2):
                value = dec[k, half][0:1, :] * sib[k, half].astype(F32) + local[k, half].astype(F32)
                chip[k, half] = value

                @pl.when(y == 0)
                def _(half=half, value=value):
                    isend[k, half] = value.astype(BF16)
                    link(k, half).start()

            return carry

        lax.fori_loop(0, PER_GROUP, one, 0)

    own_state(0)
    pl.semaphore_wait(barrier, 3)

    @pl.when(c == 0)
    def _():
        ex_d(0).start()
        ex_state(0).start()

    def send_own(parts):
        for e in parts:
            @pl.when(down_sends(e))
            def _(e=e):
                down_copy(e)[0].start()

            @pl.when(up_sends(e) & (y > 0))
            def _(e=e):
                up_copy(e)[0].start()

    for i in range(2):
        own_sib(i).start()

    @pl.when(c == 0)
    def _():
        send_own((0, 2))

    for g in range(1, GROUPS):
        own_state(g)

        @pl.when(c == 0)
        def _(g=g):
            ex_d(g).start()
            ex_state(g).start()

        @pl.when(c == 1)
        def _(g=g):
            chip_state(g - 1)

    @pl.when(c == 1)
    def _():
        chip_state(GROUPS - 1)

    @pl.when(y == 0)
    def _():
        pin[0 : CHUNKS - 1] = jnp.zeros((CHUNKS - 1, 2, BLK, PIECE), BF16)

    @pl.when((y == 0) & (c == 1))
    def _():
        pin[CHUNKS - 1] = jnp.zeros((2, BLK, PIECE), BF16)

    @pl.when(c == 0)
    def _():
        for i in range(2):
            own_sib(i).wait_recv()
        send_own((1, 3))

    for load in loads[7:]:
        load.wait()

    def own_part(j):
        g = lax.div(j, 2)
        cols = pl.ds(pl.multiple_of(j * HALF, HALF), HALF)
        state_cols = pl.ds(pl.multiple_of(g * BLK, BLK), BLK)
        wide = dot(stack[BLK + 32 : 2 * BLK + 64, :], spread[j])
        uu = wide[0:BLK]
        sk = wide[BLK : BLK + 1] + wide[BLK + 16 : BLK + 17]
        products = dot_t(cp[:, state_cols], b[:, state_cols])
        mixing = jnp.where(tri, products, 0.0).astype(BF16)
        base = uu * dot(mixing, xs[:, cols]) + sk * x[:, cols].astype(F32)
        gt = gate[:, cols].astype(F32)
        act = gt / (1.0 + jnp.exp(-gt))
        a1[:, cols] = base * act
        a2[:, cols] = uu * act

    def attention(piece):
        blocks = [lists[0, i] for i in range(3)]
        slots = [me] + [jnp.where(i < 0, me, i) for i in blocks]
        biases = [jnp.where(i < 0, MASKED, 0.0).astype(F32) for i in blocks]
        tris = jnp.concatenate([tri] * RATIO, axis=0)
        scale = HEAD_D ** (-0.5) * LOG2_E
        for h in range(ATTN_KEY_HEADS):
            kh = piece * ATTN_KEY_HEADS + h
            cols = pl.ds(pl.multiple_of(kh * HEAD_D, HEAD_D), HEAD_D)
            heads = [pl.ds(pl.multiple_of((kh * RATIO + i) * HEAD_D, HEAD_D), HEAD_D) for i in range(RATIO)]
            queries = jnp.concatenate([q[:, head] for head in heads], axis=0)
            keys = jnp.concatenate([kv[slot, 0, :, cols] for slot in slots], axis=0)
            values = jnp.concatenate([kv[slot, 1, :, cols] for slot in slots], axis=0)
            values = jnp.concatenate([values, jnp.ones(values.shape, BF16)], axis=1)
            scores = dot_t(queries, keys)
            scores = [scores[:, i * BLK : (i + 1) * BLK] for i in range(4)]
            scores = [jnp.where(tris, scores[0], MASKED)] + [s + bias for s, bias in zip(scores[1:], biases)]
            top = jnp.maximum(jnp.maximum(scores[0], scores[1]), jnp.maximum(scores[2], scores[3]))
            top = jnp.max(top, axis=1, keepdims=True)
            weights = jnp.concatenate([jnp.exp2((s - top) * scale).astype(BF16) for s in scores], axis=1)
            acc = dot(weights, values)
            out = (acc[:, :HEAD_D] / acc[:, HEAD_D:]).astype(BF16)
            for i, head in enumerate(heads):
                attn_v[:, head] = out[i * BLK : (i + 1) * BLK]

    def psib(k):
        return remote(pin.at[k], pin.at[k], psib_s.at[0], psib_r.at[k], other)

    late = (y >= 2) & (y <= 4)

    def finish(g):
        cols = pl.ds(pl.multiple_of(g * COLS, COLS), COLS)
        state_cols = pl.ds(pl.multiple_of(g * BLK, BLK), BLK)

        @pl.when((y > 0) & (c == 0))
        def _():
            for i in range(PER_GROUP - 1):
                psib(g * PER_GROUP + i).wait_recv()

            @pl.when(jnp.logical_not(late) | (g < GROUPS - 1))
            def _():
                psib((g + 1) * PER_GROUP - 1).wait_recv()

        def part(state):
            gated = a1[:, cols] + a2[:, cols] * dot(cp[:, state_cols], state)
            square = jnp.sum(gated * gated, axis=1, keepdims=True)
            scale = lax.rsqrt(square * (1.0 / COLS) + NORM_EPS)
            ssm_v[:, cols] = (gated * scale * gain[:, cols]).astype(BF16)

        def entering(half, i):
            k = g * PER_GROUP + i
            came = pin[k, half].astype(F32)
            return (dsib[k, half][0:1, :] * came + sib[k, half].astype(F32)).astype(BF16)

        pieces = [(half, i) for half in range(2) for i in range(PER_GROUP)]

        @pl.when(c == 0)
        def _():
            part(jnp.concatenate([pin[g * PER_GROUP + i, half] for half, i in pieces], axis=1))

        @pl.when(c == 1)
        def _():
            part(jnp.concatenate([entering(half, i) for half, i in pieces], axis=1))


    reach = lax.div(y * LAG_NUM, LAG_DEN)
    attn_at = pick(y, ATTN_TICK)
    norm_at = pick(y, NORM_TICK)
    last_chip = y == CHIPS - 1
    behind = jnp.where(last_chip, CHUNKS + 2, CHUNKS + 1 + GROUPS)
    end = jnp.maximum(reach + behind, attn_at + ATTN_PIECES)
    late_from = (y >= 1) & (y <= 5)
    late_event = jnp.where(y == 1, 0, jnp.where(y == 5, KV_PARTS + 2, KV_PARTS))

    def tick(t, carry):
        k = t - reach

        @pl.when((c == 1) & (y > 0) & (k >= 0) & (k < CHUNKS))
        def _():
            for half in range(2):
                link(k, half).wait_recv()

                @pl.when(y < CHIPS - 1)
                def _(half=half):
                    d = dec[k, half][0:1, :] * dsib[k, half][0:1, :]
                    isend[k, half] = (d * pin[k, half].astype(F32) + chip[k, half]).astype(BF16)
                    link(k, half).start()

            psib(k).start()

        @pl.when(t < GROUPS)
        def _():
            own_part(2 * t)
            own_part(2 * t + 1)

        @pl.when((y == 0) & (t == FIRST_TICK))
        def _():
            @pl.when(c == 1)
            def _():
                remote(isend, pin, chain_s.at[0], chain_r.at[0], above).wait_send()
                psib(CHUNKS - 1).start()

            @pl.when(c == 0)
            def _():
                psib(CHUNKS - 1).wait_recv()
                for e in range(KV_PARTS):
                    up_copy(e)[0].start()

        @pl.when((c == 0) & late & (t == norm_at))
        def _():
            psib(CHUNKS - 1).wait_recv()
            for e in range(KV_PARTS, 2 * KV_PARTS):
                @pl.when((y < 4) | (e >= KV_PARTS + 2))
                def _(e=e):
                    up_copy(e)[0].start()

        @pl.when(t == norm_at)
        def _():
            for g in range(GROUPS - 1):
                finish(g)

        @pl.when(t == jnp.where(last_chip, reach + CHUNKS + 1, norm_at))
        def _():
            finish(GROUPS - 1)

        e = lax.div(t - KV_FIRST + KV_TICKS, KV_TICKS) - 1
        now = (c == 0) & (lax.rem(t, KV_TICKS) == 0) & (t >= KV_FIRST)

        @pl.when(now & (e < KV_PARTS * DOWN_STEPS) & down_gets(jnp.maximum(e, 0)))
        def _():
            arrival, piece = down_copy(e, 1)
            arrival.wait_recv()

            @pl.when((e < KV_PARTS * (DOWN_STEPS - 1)) & down_sends(e + KV_PARTS))
            def _():
                down_copy(e + KV_PARTS)[0].start()

            @pl.when(down_keeps(e))
            def _():
                kv_sib(DOWN0 + e, piece).start()

        behind = (c == 0) & late_from & (k > CHUNKS + LATE) & (k <= CHUNKS + LATE + KV_PARTS)
        u = jnp.where(behind, k - CHUNKS - LATE - 1 + late_event, e)
        due = behind | (now & (e < KV_PARTS * UP_STEPS) & (jnp.logical_not(late_from) | (e < late_event)))

        @pl.when(due & up_gets(jnp.maximum(u, 0)))
        def _():
            arrival, piece = up_copy(u, 1)
            arrival.wait_recv()

            @pl.when((u < KV_PARTS * (UP_STEPS - 1)) & up_sends(u + KV_PARTS) & (jnp.logical_not(late) | ((y == 4) & (u < 2))))
            def _():
                up_copy(u + KV_PARTS)[0].start()

            kv_sib(UP0 + u, piece).start()

        @pl.when((t == attn_at) & (c == 0))
        def _():
            for g in range(GROUPS):
                ex_d(g).wait_send()
                ex_state(g).wait_send()

            def wait_up_sent(i, carry):
                @pl.when(up_sends(i))
                def _():
                    up_copy(i)[0].wait_send()

                @pl.when(up_gets(i))
                def _():
                    kv_sib(UP0 + i, kv.at[me, 0]).wait_send()
                return carry

            def wait_down_sent(i, carry):
                @pl.when(down_sends(i))
                def _():
                    down_copy(i)[0].wait_send()

                @pl.when(down_keeps(i))
                def _():
                    kv_sib(DOWN0 + i, kv.at[me, 0]).wait_send()
                return carry

            lax.fori_loop(0, KV_PARTS * UP_STEPS, wait_up_sent, 0)
            lax.fori_loop(0, KV_PARTS * DOWN_STEPS, wait_down_sent, 0)
            for i in range(2):
                own_sib(i).wait_send()

        @pl.when((t == attn_at) & (c == 1))
        def _():
            for i in range(2):
                own_sib(i).wait()

            def wait_up(i, carry):
                @pl.when(up_gets(i))
                def _():
                    kv_sib(UP0 + i, kv.at[me, 0]).wait_recv()
                return carry

            def wait_down(i, carry):
                @pl.when(down_keeps(i))
                def _():
                    kv_sib(DOWN0 + i, kv.at[me, 0]).wait_recv()
                return carry

            lax.fori_loop(0, KV_PARTS * UP_STEPS, wait_up, 0)
            lax.fori_loop(0, KV_PARTS * DOWN_STEPS, wait_down, 0)

        @pl.when((t >= attn_at) & (t < attn_at + ATTN_PIECES))
        def _():
            attention(t - attn_at)

        return carry

    lax.fori_loop(0, end, tick, 0)

    @pl.when((y > 0) & (c == 1))
    def _():
        remote(pin, pin, psib_s.at[0], psib_r.at[0], other).wait_send()

    @pl.when((y > 0) & (y < CHIPS - 1) & (c == 1))
    def _():
        remote(isend, pin, chain_s.at[0], chain_r.at[0], above).wait_send()

    @pl.when((y == 0) & (c == 1))
    def _():
        psib(CHUNKS - 1).wait_send()


def store_kernel(ssm, attn, ssm_out, attn_out, sem):
    copies = []
    for src, dst in ((ssm, ssm_out), (attn, attn_out)):
        for i in range(STORES):
            rows = pl.ds(i * (BLK // STORES), BLK // STORES)
            copies.append(pltpu.make_async_copy(src.at[rows], dst.at[rows], sem.at[len(copies)]))
    for copy in copies:
        copy.start()
    for copy in copies:
        copy.wait()


def body(ssm_input, gate_input, b_proj, c_proj, dt_raw, a_log, skip, norm_gain, queries, keys, values, block_lists):
    vmem = pltpu.VMEM
    dma = lambda n: pltpu.SemaphoreType.DMA((n,))
    wide = GROUPS * COLS
    heads = KVHEADS * RATIO * HEAD_D
    any_spec = pl.BlockSpec(memory_space=pl.ANY)
    vmem_spec = pl.BlockSpec(memory_space=pltpu.VMEM)
    outs = (jax.ShapeDtypeStruct((BLK, wide), BF16), jax.ShapeDtypeStruct((BLK, heads), BF16))
    ssm, attn = pl.pallas_call(
        kernel,
        out_shape=(vmem((BLK, wide), BF16), vmem((BLK, heads), BF16)),
        in_specs=[any_spec] * 12,
        out_specs=(vmem_spec, vmem_spec),
        scratch_shapes=[
            vmem((BLK, wide), BF16), vmem((BLK, wide), BF16), vmem((BLK, GROUPS * BLK), BF16),
            vmem((BLK, GROUPS * BLK), BF16), vmem((SSM_HEADS, BLK), F32), vmem((1, SSM_HEADS), F32),
            vmem((1, SSM_HEADS), F32), vmem((1, wide), F32), vmem((BLK, heads), BF16),
            pltpu.SMEM((1, 3), jnp.int32),
            vmem((2 * CHIPS, 2, BLK, KVHEADS * HEAD_D), BF16),
            vmem((2 * BLK + 64, SSM_HEADS), BF16), vmem((2 * GROUPS, SSM_HEADS, HALF), BF16),
            vmem((GROUPS, BLK, BLK), BF16),
            vmem((BLK, wide), BF16), vmem((BLK, wide), F32), vmem((BLK, wide), F32),
            vmem((CHUNKS, 2, BLK, PIECE), BF16), vmem((CHUNKS, 2, BLK, PIECE), BF16),
            vmem((CHUNKS, 2, 8, PIECE), F32), vmem((CHUNKS, 2, 8, PIECE), F32),
            vmem((CHUNKS, 2, BLK, PIECE), F32), vmem((CHUNKS, 2, BLK, PIECE), BF16),
            vmem((CHUNKS, 2, BLK, PIECE), BF16),
            dma(12),
            dma(KV_PARTS * UP_STEPS), dma(KV_PARTS * UP_STEPS), dma(KV_PARTS * DOWN_STEPS),
            dma(KV_PARTS * DOWN_STEPS), dma(2 + KV_PARTS * (UP_STEPS + DOWN_STEPS)),
            dma(2 + KV_PARTS * (UP_STEPS + DOWN_STEPS)),
            dma(1), dma(2 * CHUNKS), dma(1), dma(CHUNKS), dma(2 * GROUPS), dma(2 * GROUPS),
        ],
        compiler_params=pltpu.CompilerParams(
            collective_id=0, has_side_effects=True, vmem_limit_bytes=60 * 2**20
        ),
        name="layers",
    )(
        ssm_input, gate_input, b_proj, c_proj, dt_raw.T, a_log.reshape(1, -1), skip.reshape(1, -1),
        norm_gain.reshape(1, -1), queries, keys, values, block_lists,
    )
    return pl.pallas_call(
        store_kernel,
        out_shape=outs,
        in_specs=[vmem_spec] * 2,
        out_specs=(any_spec, any_spec),
        scratch_shapes=[dma(2 * STORES)],
        compiler_params=pltpu.CompilerParams(vmem_limit_bytes=4 * 2**20),
        name="store",
    )(ssm, attn)


def solution(mesh):
    rows = P(("dp", "ctx"), None)
    in_specs = (rows, rows, rows, rows, rows, P(), P(), P(), rows, rows, rows, rows)
    return jax.shard_map(body, mesh=mesh, in_specs=in_specs, out_specs=(rows, rows), check_vma=False)
```

```python
import jax
import jax.numpy as jnp
from jax import lax
from jax.experimental import pallas as pl
from jax.experimental.pallas import tpu as pltpu
from jax.sharding import PartitionSpec as P

MESH = pl.DeviceIdType.MESH
F32 = jnp.float32
BF16 = jnp.bfloat16

SSM_HEADS = 64
HEAD_P = 64
GROUPS = 4
KVHEADS = 4
RATIO = 4
HEAD_D = 128
BLK = 128
NORM_EPS = 1e-05
MASKED = -1e30
LOG2_E = 1.4426950408889634

CHIPS = 8
HALF = 512
COLS = 1024
PIECE = 128
PER_GROUP = 4
CHUNKS = GROUPS * PER_GROUP
UP_STEPS = 3
DOWN_STEPS = 5
LAG_NUM, LAG_DEN = 7, 2
KV_PARTS = 4
KV_TICKS = 2
KV_FIRST = 4
LATE = 4
FIRST_TICK = 22
NORM_TICK = (23, 23, 23, 26, 34, 38, 37, 35)
ATTN_TICK = (32, 28, 31, 43, 43, 43, 43, 39)
ATTN_KEY_HEADS = 4
STORES = 2
ATTN_PIECES = KVHEADS // ATTN_KEY_HEADS


def dot(a, b):
    return lax.dot_general(a, b, (((1,), (0,)), ((), ())), preferred_element_type=F32)


def dot_t(a, b):
    return lax.dot_general(a, b, (((1,), (1,)), ((), ())), preferred_element_type=F32)


def split(v):
    hi = v.astype(BF16)
    return hi, (v - hi.astype(F32)).astype(BF16)


def pick(y, table):
    value = table[0]
    for i in range(1, CHIPS):
        value = jnp.where(y == i, table[i], value)
    return value


def kernel(
    x_hbm, gate_hbm, b_hbm, c_hbm, dt_hbm, alog_hbm, skip_hbm, gain_hbm, q_hbm, k_hbm, v_hbm, list_hbm,
    ssm_v, attn_v,
    x, gate, b, cp, dtr, alog, skip, gain, q, lists,
    kv, stack, spread, xs, a1, a2, local, sib, dec, dsib, chip, isend, pin,
    in_sem,
    up_s, up_r, down_s, down_r, kvsib_s, kvsib_r, chain_s, chain_r, psib_s, psib_r, ex_s, ex_r,
):
    me = lax.axis_index("ctx")
    y = lax.div(me, 2)
    c = lax.rem(me, 2)
    oc = 1 - c
    above = lax.rem(y + 1, CHIPS) * 2 + c
    below = lax.rem(y + CHIPS - 1, CHIPS) * 2 + c
    other = y * 2 + oc

    barrier = pltpu.get_barrier_semaphore()
    for peer in (above, below, other):
        pl.semaphore_signal(barrier, inc=1, device_id={"ctx": peer}, device_id_type=MESH)

    loads = [
        pltpu.make_async_copy(src, dst, in_sem.at[i])
        for i, (src, dst) in enumerate(
            (
                (dt_hbm, dtr), (alog_hbm, alog), (skip_hbm, skip), (b_hbm, b),
                (k_hbm, kv.at[me, 0]), (v_hbm, kv.at[me, 1]), (x_hbm, x), (c_hbm, cp), (gate_hbm, gate),
                (gain_hbm, gain), (q_hbm, q), (list_hbm, lists),
            )
        )
    ]
    for load in loads:
        load.start()

    def remote(src, dst, send, recv, to):
        return pltpu.make_async_remote_copy(
            src_ref=src, dst_ref=dst, send_sem=send, recv_sem=recv, device_id={"ctx": to}, device_id_type=MESH
        )

    def kv_piece(chip_y, part):
        return kv.at[chip_y * 2 + lax.rem(part, 2), lax.div(part, 2)]

    def up_copy(e, ahead=0):
        from_y = lax.rem(y - ahead - lax.div(e, KV_PARTS) + CHIPS, CHIPS)
        piece = kv_piece(from_y, lax.rem(e, KV_PARTS))
        return remote(piece, piece, up_s.at[e], up_r.at[e], above), piece

    def down_copy(e, ahead=0):
        from_y = lax.rem(y + ahead + lax.div(e, KV_PARTS), CHIPS)
        piece = kv_piece(from_y, lax.rem(e, KV_PARTS))
        return remote(piece, piece, down_s.at[e], down_r.at[e], below), piece

    def up_goes(source, e):
        values = lax.rem(e, KV_PARTS) >= KV_PARTS // 2
        return (e < 2 * KV_PARTS) | ((source >= 4) & values)

    def down_goes(source, e):
        keys = lax.rem(e, KV_PARTS) < KV_PARTS // 2
        return (source < 4) | ((source == 4) & keys)

    def up_sends(e):
        step = lax.div(e, KV_PARTS)
        return (y < CHIPS - 1) & (y >= step) & up_goes(y - step, e)

    def up_gets(e):
        step = lax.div(e, KV_PARTS)
        return (y >= 1 + step) & up_goes(y - 1 - step, e)

    def down_sends(e):
        step = lax.div(e, KV_PARTS)
        return down_goes(lax.rem(y + step, CHIPS), e)

    def down_gets(e):
        step = lax.div(e, KV_PARTS)
        return down_goes(lax.rem(y + 1 + step, CHIPS), e)

    def down_keeps(e):
        return (y + 1 + lax.div(e, KV_PARTS) >= CHIPS) & down_gets(e)

    def kv_sib(i, piece):
        return remote(piece, piece, kvsib_s.at[i], kvsib_r.at[i], other)

    def own_sib(i):
        return kv_sib(i, kv.at[me, i])

    UP0, DOWN0 = 2, 2 + KV_PARTS * UP_STEPS

    r = lax.broadcasted_iota(jnp.int32, (SSM_HEADS, HALF), 0)
    h = lax.shift_right_logical(lax.broadcasted_iota(jnp.int32, (SSM_HEADS, HALF), 1), 6)
    for j in range(2 * GROUPS):
        spread[j] = (r - j * (HALF // HEAD_P) == h).astype(F32).astype(BF16)

    for load in loads[:4]:
        load.wait()
    raw = jnp.transpose(dtr[...])
    dt = jnp.maximum(raw, 0.0) + jnp.log1p(jnp.exp(-jnp.abs(raw)))
    rate = jnp.exp(alog[...])
    row = lax.broadcasted_iota(jnp.int32, (BLK, BLK), 0)
    col = lax.broadcasted_iota(jnp.int32, (BLK, BLK), 1)
    tri = row >= col
    cum = lax.dot_general(
        tri.astype(F32), -dt * rate, (((1,), (0,)), ((), ())), precision=lax.Precision.HIGHEST,
        preferred_element_type=F32,
    )
    up_to = jnp.exp(cum)
    l_hi, l_lo = split(jnp.broadcast_to(up_to[BLK - 1 : BLK], (16, SSM_HEADS)))
    s_hi, s_lo = split(jnp.broadcast_to(skip[...], (16, SSM_HEADS)))
    stack[0:BLK, :] = (dt * jnp.exp(-cum)).astype(BF16)
    stack[BLK : BLK + 16, :] = l_hi
    stack[BLK + 16 : BLK + 32, :] = l_lo
    stack[BLK + 32 : 2 * BLK + 32, :] = up_to.astype(BF16)
    stack[2 * BLK + 32 : 2 * BLK + 48, :] = s_hi
    stack[2 * BLK + 48 : 2 * BLK + 64, :] = s_lo
    for load in loads[4:7]:
        load.wait()

    def ex_d(g):
        some = pl.ds(g * PER_GROUP, PER_GROUP)
        return remote(dec.at[some], dsib.at[some], ex_s.at[g], ex_r.at[g], other)

    def ex_state(g):
        some = pl.ds(g * PER_GROUP, PER_GROUP)
        i = GROUPS + g
        return remote(local.at[some], sib.at[some], ex_s.at[i], ex_r.at[i], other)

    def link(k, half):
        n = k * 2 + half
        return remote(isend.at[k, half], pin.at[k, half], chain_s.at[0], chain_r.at[n], above)

    def own_state(g):
        bt = jnp.transpose(b[:, g * BLK : (g + 1) * BLK].astype(F32)).astype(BF16)
        for half in range(2):
            j = 2 * g + half
            cols = pl.ds(j * HALF, HALF)
            wide = dot(stack[0 : BLK + 32, :], spread[j])
            scaled = (x[:, cols].astype(F32) * wide[0:BLK]).astype(BF16)
            xs[:, cols] = scaled
            last = wide[BLK : BLK + 1] + wide[BLK + 16 : BLK + 17]
            state = dot(bt, scaled) * last
            for i in range(PER_GROUP):
                piece = slice(i * PIECE, (i + 1) * PIECE)
                local[g * PER_GROUP + i, half] = state[:, piece].astype(BF16)
                dec[g * PER_GROUP + i, half] = jnp.broadcast_to(last[:, piece], (8, PIECE))

    def chip_state(g):
        ex_d(g).wait_recv()
        ex_state(g).wait_recv()

        def one(i, carry):
            k = g * PER_GROUP + i
            for half in range(2):
                value = dec[k, half][0:1, :] * sib[k, half].astype(F32) + local[k, half].astype(F32)
                chip[k, half] = value

                @pl.when(y == 0)
                def _(half=half, value=value):
                    isend[k, half] = value.astype(BF16)
                    link(k, half).start()

            return carry

        lax.fori_loop(0, PER_GROUP, one, 0)

    own_state(0)
    pl.semaphore_wait(barrier, 3)

    @pl.when(c == 0)
    def _():
        ex_d(0).start()
        ex_state(0).start()

    def send_own(parts):
        for e in parts:
            @pl.when(down_sends(e))
            def _(e=e):
                down_copy(e)[0].start()

            @pl.when(up_sends(e) & (y > 0))
            def _(e=e):
                up_copy(e)[0].start()

    for i in range(2):
        own_sib(i).start()

    @pl.when(c == 0)
    def _():
        send_own((0, 2))

    for g in range(1, GROUPS):
        own_state(g)

        @pl.when(c == 0)
        def _(g=g):
            ex_d(g).start()
            ex_state(g).start()

        @pl.when(c == 1)
        def _(g=g):
            chip_state(g - 1)

        if g == 2:
            @pl.when(c == 0)
            def _():
                for i in range(2):
                    own_sib(i).wait_recv()
                send_own((1, 3))

    @pl.when(c == 1)
    def _():
        chip_state(GROUPS - 1)

    @pl.when(y == 0)
    def _():
        pin[0 : CHUNKS - 1] = jnp.zeros((CHUNKS - 1, 2, BLK, PIECE), BF16)

    @pl.when((y == 0) & (c == 1))
    def _():
        pin[CHUNKS - 1] = jnp.zeros((2, BLK, PIECE), BF16)


    for load in loads[7:]:
        load.wait()

    def own_part(j):
        g = lax.div(j, 2)
        cols = pl.ds(pl.multiple_of(j * HALF, HALF), HALF)
        state_cols = pl.ds(pl.multiple_of(g * BLK, BLK), BLK)
        wide = dot(stack[BLK + 32 : 2 * BLK + 64, :], spread[j])
        uu = wide[0:BLK]
        sk = wide[BLK : BLK + 1] + wide[BLK + 16 : BLK + 17]
        products = dot_t(cp[:, state_cols], b[:, state_cols])
        mixing = jnp.where(tri, products, 0.0).astype(BF16)
        base = uu * dot(mixing, xs[:, cols]) + sk * x[:, cols].astype(F32)
        gt = gate[:, cols].astype(F32)
        act = gt / (1.0 + jnp.exp(-gt))
        a1[:, cols] = base * act
        a2[:, cols] = uu * act

    def attention(piece):
        blocks = [lists[0, i] for i in range(3)]
        slots = [me] + [jnp.where(i < 0, me, i) for i in blocks]
        biases = [jnp.where(i < 0, MASKED, 0.0).astype(F32) for i in blocks]
        tris = jnp.concatenate([tri] * RATIO, axis=0)
        scale = HEAD_D ** (-0.5) * LOG2_E
        for h in range(ATTN_KEY_HEADS):
            kh = piece * ATTN_KEY_HEADS + h
            cols = pl.ds(pl.multiple_of(kh * HEAD_D, HEAD_D), HEAD_D)
            heads = [pl.ds(pl.multiple_of((kh * RATIO + i) * HEAD_D, HEAD_D), HEAD_D) for i in range(RATIO)]
            queries = jnp.concatenate([q[:, head] for head in heads], axis=0)
            keys = jnp.concatenate([kv[slot, 0, :, cols] for slot in slots], axis=0)
            values = jnp.concatenate([kv[slot, 1, :, cols] for slot in slots], axis=0)
            values = jnp.concatenate([values, jnp.ones(values.shape, BF16)], axis=1)
            scores = dot_t(queries, keys)
            scores = [scores[:, i * BLK : (i + 1) * BLK] for i in range(4)]
            scores = [jnp.where(tris, scores[0], MASKED)] + [s + bias for s, bias in zip(scores[1:], biases)]
            top = jnp.maximum(jnp.maximum(scores[0], scores[1]), jnp.maximum(scores[2], scores[3]))
            top = jnp.max(top, axis=1, keepdims=True)
            weights = jnp.concatenate([jnp.exp2((s - top) * scale).astype(BF16) for s in scores], axis=1)
            acc = dot(weights, values)
            out = (acc[:, :HEAD_D] / acc[:, HEAD_D:]).astype(BF16)
            for i, head in enumerate(heads):
                attn_v[:, head] = out[i * BLK : (i + 1) * BLK]

    def psib(k):
        return remote(pin.at[k], pin.at[k], psib_s.at[0], psib_r.at[k], other)

    late = (y >= 2) & (y <= 4)

    def finish(g):
        cols = pl.ds(pl.multiple_of(g * COLS, COLS), COLS)
        state_cols = pl.ds(pl.multiple_of(g * BLK, BLK), BLK)

        @pl.when((y > 0) & (c == 0))
        def _():
            for i in range(PER_GROUP - 1):
                psib(g * PER_GROUP + i).wait_recv()

            @pl.when(jnp.logical_not(late) | (g < GROUPS - 1))
            def _():
                psib((g + 1) * PER_GROUP - 1).wait_recv()

        def part(state):
            gated = a1[:, cols] + a2[:, cols] * dot(cp[:, state_cols], state)
            square = jnp.sum(gated * gated, axis=1, keepdims=True)
            scale = lax.rsqrt(square * (1.0 / COLS) + NORM_EPS)
            ssm_v[:, cols] = (gated * scale * gain[:, cols]).astype(BF16)

        def entering(half, i):
            k = g * PER_GROUP + i
            came = pin[k, half].astype(F32)
            return (dsib[k, half][0:1, :] * came + sib[k, half].astype(F32)).astype(BF16)

        pieces = [(half, i) for half in range(2) for i in range(PER_GROUP)]

        @pl.when(c == 0)
        def _():
            part(jnp.concatenate([pin[g * PER_GROUP + i, half] for half, i in pieces], axis=1))

        @pl.when(c == 1)
        def _():
            part(jnp.concatenate([entering(half, i) for half, i in pieces], axis=1))


    reach = lax.div(y * LAG_NUM, LAG_DEN)
    attn_at = pick(y, ATTN_TICK)
    norm_at = pick(y, NORM_TICK)
    last_chip = y == CHIPS - 1
    behind = jnp.where(last_chip, CHUNKS + 2, CHUNKS + 1 + GROUPS)
    end = jnp.maximum(reach + behind, attn_at + ATTN_PIECES)
    late_from = (y >= 1) & (y <= 5)
    late_event = jnp.where(y == 1, 0, jnp.where(y == 5, KV_PARTS + 2, KV_PARTS))

    def tick(t, carry):
        k = t - reach

        @pl.when((c == 1) & (y > 0) & (k >= 0) & (k < CHUNKS))
        def _():
            for half in range(2):
                link(k, half).wait_recv()

                @pl.when(y < CHIPS - 1)
                def _(half=half):
                    d = dec[k, half][0:1, :] * dsib[k, half][0:1, :]
                    isend[k, half] = (d * pin[k, half].astype(F32) + chip[k, half]).astype(BF16)
                    link(k, half).start()

            psib(k).start()

        @pl.when(t < GROUPS)
        def _():
            own_part(2 * t)
            own_part(2 * t + 1)

        @pl.when((y == 0) & (t == FIRST_TICK))
        def _():
            @pl.when(c == 1)
            def _():
                remote(isend, pin, chain_s.at[0], chain_r.at[0], above).wait_send()
                psib(CHUNKS - 1).start()

            @pl.when(c == 0)
            def _():
                psib(CHUNKS - 1).wait_recv()
                for e in range(KV_PARTS):
                    up_copy(e)[0].start()

        @pl.when((c == 0) & late & (t == norm_at))
        def _():
            psib(CHUNKS - 1).wait_recv()
            for e in range(KV_PARTS, 2 * KV_PARTS):
                @pl.when((y < 4) | (e >= KV_PARTS + 2))
                def _(e=e):
                    up_copy(e)[0].start()

        @pl.when(t == norm_at)
        def _():
            for g in range(GROUPS - 1):
                finish(g)

        @pl.when(t == jnp.where(last_chip, reach + CHUNKS + 1, norm_at))
        def _():
            finish(GROUPS - 1)

        e = lax.div(t - KV_FIRST + KV_TICKS, KV_TICKS) - 1
        now = (c == 0) & (lax.rem(t, KV_TICKS) == 0) & (t >= KV_FIRST)

        @pl.when(now & (e < KV_PARTS * DOWN_STEPS) & down_gets(jnp.maximum(e, 0)))
        def _():
            arrival, piece = down_copy(e, 1)
            arrival.wait_recv()

            @pl.when((e < KV_PARTS * (DOWN_STEPS - 1)) & down_sends(e + KV_PARTS))
            def _():
                down_copy(e + KV_PARTS)[0].start()

            @pl.when(down_keeps(e))
            def _():
                kv_sib(DOWN0 + e, piece).start()

        behind = (c == 0) & late_from & (k > CHUNKS + LATE) & (k <= CHUNKS + LATE + KV_PARTS)
        u = jnp.where(behind, k - CHUNKS - LATE - 1 + late_event, e)
        due = behind | (now & (e < KV_PARTS * UP_STEPS) & (jnp.logical_not(late_from) | (e < late_event)))

        @pl.when(due & up_gets(jnp.maximum(u, 0)))
        def _():
            arrival, piece = up_copy(u, 1)
            arrival.wait_recv()

            @pl.when((u < KV_PARTS * (UP_STEPS - 1)) & up_sends(u + KV_PARTS) & (jnp.logical_not(late) | ((y == 4) & (u < 2))))
            def _():
                up_copy(u + KV_PARTS)[0].start()

            kv_sib(UP0 + u, piece).start()

        @pl.when((t == attn_at) & (c == 0))
        def _():
            for g in range(GROUPS):
                ex_d(g).wait_send()
                ex_state(g).wait_send()

            def wait_up_sent(i, carry):
                @pl.when(up_sends(i))
                def _():
                    up_copy(i)[0].wait_send()

                @pl.when(up_gets(i))
                def _():
                    kv_sib(UP0 + i, kv.at[me, 0]).wait_send()
                return carry

            def wait_down_sent(i, carry):
                @pl.when(down_sends(i))
                def _():
                    down_copy(i)[0].wait_send()

                @pl.when(down_keeps(i))
                def _():
                    kv_sib(DOWN0 + i, kv.at[me, 0]).wait_send()
                return carry

            lax.fori_loop(0, KV_PARTS * UP_STEPS, wait_up_sent, 0)
            lax.fori_loop(0, KV_PARTS * DOWN_STEPS, wait_down_sent, 0)
            for i in range(2):
                own_sib(i).wait_send()

        @pl.when((t == attn_at) & (c == 1))
        def _():
            for i in range(2):
                own_sib(i).wait()

            def wait_up(i, carry):
                @pl.when(up_gets(i))
                def _():
                    kv_sib(UP0 + i, kv.at[me, 0]).wait_recv()
                return carry

            def wait_down(i, carry):
                @pl.when(down_keeps(i))
                def _():
                    kv_sib(DOWN0 + i, kv.at[me, 0]).wait_recv()
                return carry

            lax.fori_loop(0, KV_PARTS * UP_STEPS, wait_up, 0)
            lax.fori_loop(0, KV_PARTS * DOWN_STEPS, wait_down, 0)

        @pl.when((t >= attn_at) & (t < attn_at + ATTN_PIECES))
        def _():
            attention(t - attn_at)

        return carry

    lax.fori_loop(0, end, tick, 0)

    @pl.when((y > 0) & (c == 1))
    def _():
        remote(pin, pin, psib_s.at[0], psib_r.at[0], other).wait_send()

    @pl.when((y > 0) & (y < CHIPS - 1) & (c == 1))
    def _():
        remote(isend, pin, chain_s.at[0], chain_r.at[0], above).wait_send()

    @pl.when((y == 0) & (c == 1))
    def _():
        psib(CHUNKS - 1).wait_send()


def store_kernel(ssm, attn, ssm_out, attn_out, sem):
    copies = []
    for src, dst in ((ssm, ssm_out), (attn, attn_out)):
        for i in range(STORES):
            rows = pl.ds(i * (BLK // STORES), BLK // STORES)
            copies.append(pltpu.make_async_copy(src.at[rows], dst.at[rows], sem.at[len(copies)]))
    for copy in copies:
        copy.start()
    for copy in copies:
        copy.wait()


def body(ssm_input, gate_input, b_proj, c_proj, dt_raw, a_log, skip, norm_gain, queries, keys, values, block_lists):
    vmem = pltpu.VMEM
    dma = lambda n: pltpu.SemaphoreType.DMA((n,))
    wide = GROUPS * COLS
    heads = KVHEADS * RATIO * HEAD_D
    any_spec = pl.BlockSpec(memory_space=pl.ANY)
    vmem_spec = pl.BlockSpec(memory_space=pltpu.VMEM)
    outs = (jax.ShapeDtypeStruct((BLK, wide), BF16), jax.ShapeDtypeStruct((BLK, heads), BF16))
    ssm, attn = pl.pallas_call(
        kernel,
        out_shape=(vmem((BLK, wide), BF16), vmem((BLK, heads), BF16)),
        in_specs=[any_spec] * 12,
        out_specs=(vmem_spec, vmem_spec),
        scratch_shapes=[
            vmem((BLK, wide), BF16), vmem((BLK, wide), BF16), vmem((BLK, GROUPS * BLK), BF16),
            vmem((BLK, GROUPS * BLK), BF16), vmem((SSM_HEADS, BLK), F32), vmem((1, SSM_HEADS), F32),
            vmem((1, SSM_HEADS), F32), vmem((1, wide), F32), vmem((BLK, heads), BF16),
            pltpu.SMEM((1, 3), jnp.int32),
            vmem((2 * CHIPS, 2, BLK, KVHEADS * HEAD_D), BF16),
            vmem((2 * BLK + 64, SSM_HEADS), BF16), vmem((2 * GROUPS, SSM_HEADS, HALF), BF16),
            vmem((BLK, wide), BF16), vmem((BLK, wide), F32), vmem((BLK, wide), F32),
            vmem((CHUNKS, 2, BLK, PIECE), BF16), vmem((CHUNKS, 2, BLK, PIECE), BF16),
            vmem((CHUNKS, 2, 8, PIECE), F32), vmem((CHUNKS, 2, 8, PIECE), F32),
            vmem((CHUNKS, 2, BLK, PIECE), F32), vmem((CHUNKS, 2, BLK, PIECE), BF16),
            vmem((CHUNKS, 2, BLK, PIECE), BF16),
            dma(12),
            dma(KV_PARTS * UP_STEPS), dma(KV_PARTS * UP_STEPS), dma(KV_PARTS * DOWN_STEPS),
            dma(KV_PARTS * DOWN_STEPS), dma(2 + KV_PARTS * (UP_STEPS + DOWN_STEPS)),
            dma(2 + KV_PARTS * (UP_STEPS + DOWN_STEPS)),
            dma(1), dma(2 * CHUNKS), dma(1), dma(CHUNKS), dma(2 * GROUPS), dma(2 * GROUPS),
        ],
        compiler_params=pltpu.CompilerParams(
            collective_id=0, has_side_effects=True, vmem_limit_bytes=60 * 2**20
        ),
        name="layers",
    )(
        ssm_input, gate_input, b_proj, c_proj, dt_raw.T, a_log.reshape(1, -1), skip.reshape(1, -1),
        norm_gain.reshape(1, -1), queries, keys, values, block_lists,
    )
    return pl.pallas_call(
        store_kernel,
        out_shape=outs,
        in_specs=[vmem_spec] * 2,
        out_specs=(any_spec, any_spec),
        scratch_shapes=[dma(2 * STORES)],
        compiler_params=pltpu.CompilerParams(vmem_limit_bytes=4 * 2**20),
        name="store",
    )(ssm, attn)


def solution(mesh):
    rows = P(("dp", "ctx"), None)
    in_specs = (rows, rows, rows, rows, rows, P(), P(), P(), rows, rows, rows, rows)
    return jax.shard_map(body, mesh=mesh, in_specs=in_specs, out_specs=(rows, rows), check_vma=False)
```
